32 devices in a mesh: tok: 8 (over z, x), head: 2 (over core), vid: 2 (over y).
Axes of the slice: x: 2, y: 2, z: 4, core: 2. Of those that a mesh axis runs over, the one named last changes fastest.
Arguments:
- queries: bfloat16 [2, 3, 1024, 2, 256], P('vid', None, 'tok', 'head'), may hold values from -6 to 6
- keys: bfloat16 [2, 3, 1024, 2, 256], P('vid', None, 'tok', 'head'), may hold values from -6 to 6
- values: bfloat16 [2, 3, 1024, 2, 256], P('vid', None, 'tok', 'head'), may hold values from -6 to 6
- out_grad: bfloat16 [2, 3, 1024, 2, 256], P('vid', None, 'tok', 'head'), may hold values from -6 to 6
- fast_init: bfloat16 [2, 3, 256, 256], P('head'), may hold values from -0.375 to 0.375
- updates: bfloat16 [2, 2, 2, 3, 256, 256], P('vid', None, 'head'), may hold values from -4 to 4
Outputs:
- query_grad: bfloat16 [2, 3, 1024, 2, 256], P('vid', None, 'tok', 'head')
- key_grad: bfloat16 [2, 3, 1024, 2, 256], P('vid', None, 'tok', 'head')
- value_grad: bfloat16 [2, 3, 1024, 2, 256], P('vid', None, 'tok', 'head')
- init_grad: float32 [2, 3, 256, 256], P('head')
The draws below stay inside these ranges and needn't reach their ends.
All inputs are finite; a program needn't handle non-finite values.
Results may differ from the reference program's by a relative error of at most 0.0014.
Values sent between devices are 32-bit elements; how exact they have to be, the bound alone decides.
No kernel may reach another device: no remote copies, remote signals or barrier semaphores. Data moves between devices by JAX's collectives and lax.ppermute only.
A program may use at most 64 MiB of HBM per device.

```python
import jax
import jax.numpy as jnp
from jax import lax

HD = 256
GROUPS = 3
HEADS = 2
VIDEOS = 2
GROUP = 1024


def steps_of(rng, dims, pieces, smallest, top_value):
    level = 1.0
    for axis_at, blocks in pieces:
        draws = jax.random.uniform(jax.random.fold_in(jax.random.fold_in(rng, 6), axis_at), (blocks,), jnp.float32, smallest / len(pieces), top_value / len(pieces))
        level = level * jnp.repeat(jnp.exp(draws), dims[axis_at] // blocks).reshape((-1,) + (1,) * (len(dims) - 1 - axis_at))
    return level


def normal_values(key, dims, deviation, bound, cuts=(), dtype=jnp.bfloat16):
    gain = steps_of(key, dims, cuts, -0.22, 0.18) if cuts else 1.0
    values = jax.random.normal(key, dims, jnp.float32) * deviation * gain
    return jnp.minimum(jnp.maximum(values, -bound), bound).astype(dtype)


def setup_inputs(seed: int = 0) -> dict:
    seeds = jax.random.split(jax.random.key(seed), 7)
    return {
        "queries": normal_values(seeds[0], (VIDEOS, GROUPS, GROUP, HEADS, HD), 1.0, 6.0, ((0, 2), (2, 8), (3, 2))),
        "keys": normal_values(seeds[1], (VIDEOS, GROUPS, GROUP, HEADS, HD), 1.0, 6.0, ((0, 2), (2, 8), (3, 2))),
        "values": normal_values(seeds[2], (VIDEOS, GROUPS, GROUP, HEADS, HD), 1.0, 6.0, ((0, 2), (2, 8), (3, 2))),
        "out_grad": normal_values(seeds[3], (VIDEOS, GROUPS, GROUP, HEADS, HD), 1.0, 6.0, ((0, 2), (2, 8), (3, 2))),
        "fast_init": normal_values(seeds[4], (HEADS, 3, HD, HD), HD ** -0.5, 0.375, ((0, 2),)),
        "updates": normal_values(seeds[5], (VIDEOS, GROUPS - 1, HEADS, 3, HD, HD), 0.5, 4.0, ((0, 2), (2, 2))),
    }


EPS = 1e-06
HIGH = lax.Precision.HIGHEST

def matmul(left, right):
    return jnp.dot(left, right, precision=HIGH, preferred_element_type=jnp.float32)

def swiglu(rows, weights):
    gate = matmul(rows, weights[0])
    upper = matmul(rows, weights[1])
    return matmul(jax.nn.silu(gate) * upper, weights[2])

def update(weights, key_rows, value_rows, scale):
    gate = matmul(key_rows, weights[0])
    upper = matmul(key_rows, weights[1])
    active = jax.nn.silu(gate)
    sigma = jax.nn.sigmoid(gate)
    down_step = matmul((active * upper).T, value_rows)
    back = matmul(value_rows, weights[2].T)
    gate_step = matmul(key_rows.T, back * upper * sigma * (1.0 + gate * (1.0 - sigma)))
    up_step = matmul(key_rows.T, back * active)
    return jnp.stack([gate_step, up_step, down_step]) * scale

def colnorm(weights, raised):
    old = jnp.sqrt(lax.optimization_barrier(jnp.sum(weights * weights, axis=-2)) + EPS)
    new = jnp.sqrt(lax.optimization_barrier(jnp.sum(raised * raised, axis=-2)) + EPS)
    return raised * (old / new)[..., None, :]

def one_pair(packed):
    init, steps, query, key_rows, value_rows, cot = packed
    scale = GROUP ** (-0.5)
    weights = [init]
    for index in range(GROUPS - 1):
        weights.append(colnorm(weights[index], weights[index] + steps[index]))
    adjoint = jnp.zeros_like(init)
    grads_q, grads_k, grads_v = ([], [], [])
    for index in reversed(range(GROUPS)):
        current = weights[index]
        if index + 1 < GROUPS:
            _, norm_back = jax.vjp(colnorm, current, current + steps[index])
            direct, upper_adj = norm_back(adjoint)
        else:
            direct = jnp.zeros_like(init)
            upper_adj = jnp.zeros_like(init)

        def local(wt, qq, kk, vv):
            return (swiglu(qq, wt), update(wt, kk, vv, scale))
        _, back = jax.vjp(local, current, query[index], key_rows[index], value_rows[index])
        wpart, dq, dk, dv = back((cot[index], upper_adj))
        adjoint = direct + upper_adj + wpart
        grads_q.append(dq)
        grads_k.append(dk)
        grads_v.append(dv)
    order = lambda items: jnp.stack(items[::-1])
    return (order(grads_q), order(grads_k), order(grads_v), adjoint)

def reference(queries, keys, values, out_grad, fast_init, updates):

    def arrange(array):
        moved = jnp.transpose(array.astype(jnp.float32), (0, 3, 1, 2, 4))
        return moved.reshape((VIDEOS * HEADS, GROUPS, GROUP, HD))
    init = jnp.broadcast_to(fast_init.astype(jnp.float32)[None], (VIDEOS, HEADS, 3, HD, HD))
    init = init.reshape((VIDEOS * HEADS, 3, HD, HD))
    steps = jnp.transpose(updates.astype(jnp.float32), (0, 2, 1, 3, 4, 5))
    steps = steps.reshape((VIDEOS * HEADS, GROUPS - 1, 3, HD, HD))
    dq, dk, dv, adjoint = lax.map(one_pair, (init, steps, arrange(queries), arrange(keys), arrange(values), arrange(out_grad)))

    def restore(array):
        shaped = array.reshape((VIDEOS, HEADS, GROUPS, GROUP, HD))
        return jnp.transpose(shaped, (0, 2, 3, 1, 4)).astype(jnp.bfloat16)
    init_grad = lax.optimization_barrier(jnp.sum(adjoint.reshape((VIDEOS, HEADS, 3, HD, HD)), axis=0))
    return (restore(dq), restore(dk), restore(dv), init_grad)
```

```python
import functools

import jax
import jax.numpy as jnp
from jax import lax
from jax.experimental import pallas as pl
from jax.experimental.pallas import tpu as pltpu
from jax.sharding import PartitionSpec as P

EPS = 1e-06
F32 = jnp.float32
BF16 = jnp.bfloat16
NN = (((1,), (0,)), ((), ()))
NT = (((1,), (1,)), ((), ()))
TN = (((0,), (0,)), ((), ()))
PAD = 8


def dot(left, right, dims):
    return lax.dot_general(left, right, dims, preferred_element_type=F32)


def split(array):
    high = array.astype(BF16)
    return high, (array - high.astype(F32)).astype(BF16)


def exact_left(left, right, dims):
    return dot(left, right[0], dims) + dot(left, right[1], dims)


def exact_right(left, right, dims):
    return dot(left[0], right, dims) + dot(left[1], right, dims)


def both_split(left, right, dims):
    return (
        dot(left[0], right[0], dims)
        + (dot(left[0], right[1], dims) + dot(left[1], right[0], dims))
    )


def silu_parts(gate):
    sigma = jax.nn.sigmoid(gate)
    rest = 1.0 - sigma
    silu = gate * sigma
    first = sigma * (1.0 + gate * rest)
    second = sigma * rest * (2.0 + gate * (1.0 - 2.0 * sigma))
    return silu, first, second


def rows_of_half(gate, up, down, which):
    dim = gate.shape[0]
    half = dim // 2
    cut = slice(which * half, (which + 1) * half)
    return [
        (0, gate[:, cut]),
        (dim, up[:, cut]),
        (2 * dim, down[cut, :half]),
        (2 * dim + half, down[cut, half:]),
    ]


def load_half(rows, dim):
    half = dim // 2
    gate_up = jnp.concatenate([rows[:dim], rows[dim : 2 * dim]], axis=1)
    down = jnp.concatenate([rows[2 * dim : 2 * dim + half], rows[2 * dim + half :]], axis=1)
    return gate_up, down


def store_parts(refs, row, value):
    size = refs[-1].shape[0]
    start = 0
    while start < value.shape[0]:
        part, inside = divmod(row + start, size)
        count = min(value.shape[0] - start, size - inside)
        refs[part][inside : inside + count, :] = value[start : start + count, :]
        start += count


def prep_kernel(init_ref, upd_ref, full_ref, mine_ref, send_ref):
    groups = upd_ref.shape[0] + 1
    dim = init_ref.shape[-1]
    half = dim // 2
    core = lax.axis_index("head") % 2
    weights = [init_ref[index].astype(F32) for index in range(3)]
    vectors = []
    levels = []
    for level in range(groups):
        levels.append(weights)
        if level + 1 == groups:
            break
        raised, ratio, cross, inverse = [], [], [], []
        for index in range(3):
            up = weights[index] + upd_ref[level, index].astype(F32)
            old2 = jnp.sum(weights[index] * weights[index], axis=0, keepdims=True) + EPS
            new2 = jnp.sum(up * up, axis=0, keepdims=True) + EPS
            old, new = jnp.sqrt(old2), jnp.sqrt(new2)
            ratio.append(old / new)
            cross.append(1.0 / (old * new))
            inverse.append(1.0 / old2)
            raised.append(up * ratio[index])
        vectors.append((ratio, cross, inverse))
        weights = raised
        for index in range(3):
            full_ref[level, index] = weights[index]

    def write(ref, which):
        cut = slice(which * half, (which + 1) * half)
        for level in range(groups):
            for row, value in rows_of_half(*levels[level], which):
                base = level * 3 * dim + row
                ref[base : base + value.shape[0], :] = value
        base = groups * 3 * dim
        for kinds in vectors:
            for gate, up, down in kinds:
                for value in (gate[:, cut], up[:, cut], down[:, :half], down[:, half:]):
                    ref[base : base + 1, :] = value
                    base += 1

    @pl.when(core == 0)
    def _():
        write(mine_ref, 0)
        write(send_ref, 1)

    @pl.when(core != 0)
    def _():
        write(mine_ref, 1)
        write(send_ref, 0)


def query_kernel(q_ref, c_ref, init_ref, full_ref, out_ref):
    groups = q_ref.shape[0]
    for index in range(groups):
        query, cot = q_ref[index], c_ref[index]
        if index == 0:
            pieces = [(init_ref[part], None) for part in range(3)]
        else:
            pieces = [split(full_ref[index - 1, part]) for part in range(3)]

        def apply(left, right, dims):
            return dot(left, right[0], dims) if right[1] is None else exact_left(left, right, dims)

        gate = apply(query, pieces[0], NN)
        up = apply(query, pieces[1], NN)
        back = apply(cot, pieces[2], NT)
        silu, first, _ = silu_parts(gate)
        total = None
        for value, piece in ((back * up * first, pieces[0]), (back * silu, pieces[1])):
            value = split(value)
            term = exact_right(value, piece[0], NT) if piece[1] is None else both_split(value, piece, NT)
            total = term if total is None else total + term
        out_ref[index] = total.astype(out_ref.dtype)


def stack_tokens(mine_ref, sib_ref, index):
    return jnp.concatenate([mine_ref[index], sib_ref[index]], axis=0).astype(BF16)


def apply_terms(query, cot, rows, dim):
    half = dim // 2
    gate_up, down = load_half(rows, dim)
    raw = exact_left(query, split(gate_up), NN)
    back = exact_left(cot, split(down), NT)
    gate, up = raw[:, :half], raw[:, half:]
    silu, first, _ = silu_parts(gate)
    grads = jnp.concatenate([back * up * first, back * silu], axis=1)
    d_gate_up = exact_left(query, split(grads), TN)
    d_down = exact_right(split(silu * up), cot, TN)
    return d_gate_up, d_down


def last_kernel(mine_ref, sib_ref, w_ref, *out_refs):
    parts, sums_ref = out_refs[:-1], out_refs[-1]
    dim = mine_ref.shape[-1]
    half = dim // 2
    query, cot = (stack_tokens(mine_ref, sib_ref, index) for index in range(2))
    d_gate_up, d_down = apply_terms(query, cot, w_ref[...], dim)
    store_parts(parts, 0, d_gate_up[:, :half])
    store_parts(parts, dim, d_gate_up[:, half:])
    sums_ref[...] = jnp.zeros_like(sums_ref)
    for block in range(2):
        value = d_down[:, block * half : (block + 1) * half]
        row = 2 * dim + block * half
        store_parts(parts, row, value)
        sums_ref[block : block + 1, :] = jnp.sum(
            value * w_ref[row : row + half, :], axis=0, keepdims=True
        )


def pre_kernel(mine_ref, sib_ref, w_ref, grad_ref, coef_ref):
    dim = mine_ref.shape[-1]
    half = dim // 2
    query, cot, key, value = (stack_tokens(mine_ref, sib_ref, index) for index in range(4))
    rows = w_ref[...]
    d_gate_up, d_down = apply_terms(query, cot, rows, dim)
    grad_ref[:dim, :] = d_gate_up[:, :half]
    grad_ref[dim : 2 * dim, :] = d_gate_up[:, half:]
    grad_ref[2 * dim : 2 * dim + half, :] = d_down[:, :half]
    grad_ref[2 * dim + half :, :] = d_down[:, half:]
    gate_up, down = load_half(rows, dim)
    raw = exact_left(key, split(gate_up), NN)
    back = exact_left(value, split(down), NT)
    gate, up = raw[:, :half], raw[:, half:]
    silu, first, second = silu_parts(gate)
    coef_ref[0] = first * up
    coef_ref[1] = silu
    coef_ref[2] = back * second * up
    coef_ref[3] = back * first
    coef_ref[4] = back * first * up
    coef_ref[5] = back * silu
    coef_ref[6] = silu * up


def key_kernel(scale, share, count, *refs):
    mine, recv = refs[:count], refs[count : 2 * count]
    tok_ref, sib_ref, new_ref, old_ref, vec_ref, grad_ref, coef_ref = refs[2 * count : 2 * count + 7]
    outs = refs[2 * count + 7 :]
    parts, (sums_ref, up_ref, mid_ref) = outs[:count], outs[count:]
    dim = tok_ref.shape[-1]
    half = dim // 2
    size = mine[-1].shape[0]
    total = jnp.concatenate([mine[j][:size] + recv[j][:size] for j in range(count)], axis=0)
    down_sums = mine[0][size:] + recv[0][size:]
    pieces = ((0, dim, 0), (dim, dim, 1), (2 * dim, half, 2), (2 * dim + half, half, 3))
    upper, carried = [], []
    for row, rows, slot in pieces:
        adj = total[row : row + rows]
        new = new_ref[row : row + rows, :]
        if slot < 2:
            sums = jnp.sum(new * adj, axis=0, keepdims=True)
        else:
            sums = down_sums[slot - 2 : slot - 1]
        ratio = vec_ref[slot : slot + 1, :]
        cross = vec_ref[4 + slot : 5 + slot, :]
        inverse = vec_ref[8 + slot : 9 + slot, :]
        up_adj = adj * ratio - new * (sums * cross)
        direct = old_ref[row : row + rows, :] * (sums * inverse)
        upper.append(up_adj * scale)
        carried.append((up_adj + direct) * share)
        up_ref[row : row + rows, :] = upper[-1]
    key, value = (stack_tokens(tok_ref, sib_ref, index) for index in (2, 3))
    raw = exact_left(key, split(jnp.concatenate(upper[:2], axis=1)), NN)
    back = exact_left(value, split(jnp.concatenate(upper[2:], axis=1)), NT)
    gate, up = raw[:, :half], raw[:, half:]
    hidden = coef_ref[0] * gate + coef_ref[1] * up
    d_gate = coef_ref[2] * gate + coef_ref[3] * up + coef_ref[0] * back
    d_up = coef_ref[3] * gate + coef_ref[1] * back
    d_gate_up = exact_left(key, split(jnp.concatenate([d_gate, d_up], axis=1)), TN)
    d_down = exact_right(split(hidden), value, TN)
    mid_ref[0] = d_gate
    mid_ref[1] = d_up
    mid_ref[2] = hidden
    store_parts(parts, 0, d_gate_up[:, :half] + grad_ref[:dim, :] + carried[0])
    store_parts(parts, dim, d_gate_up[:, half:] + grad_ref[dim : 2 * dim, :] + carried[1])
    sums_ref[...] = jnp.zeros_like(sums_ref)
    for block in range(2):
        row = 2 * dim + block * half
        out = d_down[:, block * half : (block + 1) * half]
        out = out + grad_ref[row : row + half, :] + carried[2 + block]
        store_parts(parts, row, out)
        sums_ref[block : block + 1, :] = jnp.sum(
            out * old_ref[row : row + half, :], axis=0, keepdims=True
        )


def token_kernel(mid_ref, coef_ref, w_ref, up_ref, mine_ref, sib_ref):
    dim = mine_ref.shape[-1]
    count = mine_ref.shape[1]
    w_gate_up, w_down = load_half(w_ref[...], dim)
    u_gate_up, u_down = load_half(up_ref[...], dim)
    left = jnp.concatenate([mid_ref[0], mid_ref[1]], axis=1)
    d_key = both_split(split(left), split(w_gate_up), NT)
    left = jnp.concatenate([coef_ref[4], coef_ref[5]], axis=1)
    d_key = d_key + both_split(split(left), split(u_gate_up), NT)
    left = jnp.concatenate([mid_ref[2], coef_ref[6]], axis=1)
    right = jnp.concatenate([w_down, u_down], axis=0)
    d_value = both_split(split(left), split(right), NN)
    mine_ref[0] = d_key[:count]
    mine_ref[1] = d_value[:count]
    sib_ref[0] = d_key[count:]
    sib_ref[1] = d_value[count:]


def working(tok_index, tok_count):
    return tok_index // (tok_count // 2) == lax.axis_index("head") % 2


def tokens_out_kernel(tok_count, *refs):
    key_ref, value_ref = refs[-2:]
    stays = working(lax.axis_index("tok"), tok_count)
    ins = refs[:-2]
    groups = len(ins) // 2
    for index in range(groups):

        def put(source):
            key_ref[index] = source[0].astype(key_ref.dtype)
            value_ref[index] = source[1].astype(value_ref.dtype)

        pl.when(stays)(functools.partial(put, ins[2 * index]))
        pl.when(jnp.logical_not(stays))(functools.partial(put, ins[2 * index + 1]))
    key_ref[groups] = jnp.zeros_like(key_ref[groups])
    value_ref[groups] = jnp.zeros_like(value_ref[groups])


def init_out_kernel(dims, *refs):
    out_ref = refs[-1]
    dim = out_ref.shape[-1]
    half = dim // 2
    for index in range(3):
        mine, recv = refs[2 * index], refs[2 * index + 1]
        size = mine.shape[1]
        axis, mask = dims[index]
        bit = (lax.axis_index(axis) // mask) % 2

        def put(first, second):
            for which in range(2):
                cut = slice(which * half, (which + 1) * half)
                for at, source in enumerate((first, second)):
                    if index < 2:
                        out_ref[index, at * size : (at + 1) * size, cut] = source[which]
                    else:
                        out_ref[index, cut, at * size : (at + 1) * size] = source[which]

        pl.when(bit == 0)(functools.partial(put, mine, recv))
        pl.when(bit != 0)(functools.partial(put, recv, mine))


def call(kernel, outs, *args, specs=None, flops=0):
    size = sum(a.size * a.dtype.itemsize for a in args)
    size += sum(o.size * o.dtype.itemsize for o in outs)
    kwargs = {} if specs is None else {"in_specs": specs}
    return pl.pallas_call(
        kernel,
        out_shape=outs,
        cost_estimate=pl.CostEstimate(flops=flops, bytes_accessed=size, transcendentals=0),
        compiler_params=pltpu.CompilerParams(vmem_limit_bytes=32 * 1024 * 1024),
        **kwargs,
    )(*args)


def shape(*dims, dtype=F32):
    return jax.ShapeDtypeStruct(dims, dtype)


def flip(array, axis, mask):
    count = lax.axis_size(axis)
    return lax.ppermute(array, axis, [(i, i ^ mask) for i in range(count)])


def swap_heads(array, tok_count, head_count):
    pairs = []
    for tok in range(tok_count):
        for head in range(head_count):
            if tok // (tok_count // 2) != head % 2:
                there = (tok ^ (tok_count // 2)) * head_count + (head ^ 1)
                pairs.append((tok * head_count + head, there))
    return lax.ppermute(array, ("tok", "head"), pairs)


def share_heads(array, tok_count, head_count):
    pairs = []
    for tok in range(tok_count):
        for head in range(head_count):
            if tok // (tok_count // 2) == head % 2:
                there = (tok ^ (tok_count // 2)) * head_count + head
                pairs.append((tok * head_count + head, there))
    return lax.ppermute(array, ("tok", "head"), pairs)


def bit_of(axis, mask):
    return (lax.axis_index(axis) // mask) % 2 == 1


def on_device(queries, keys, values, out_grad, fast_init, updates):
    tok_count = lax.axis_size("tok")
    head_count = lax.axis_size("head")
    vid_count = lax.axis_size("vid")
    _, groups, count, _, dim = queries.shape
    half = dim // 2
    rows = 3 * dim
    scale = float(count * tok_count) ** (-0.5)
    share = 2.0 / tok_count
    tok_masks = [1 << i for i in range((tok_count // 2).bit_length() - 1)]
    vid_masks = [1 << i for i in range(vid_count.bit_length() - 1)]
    assert len(tok_masks) >= 1 and 2 << len(tok_masks) == tok_count
    assert 1 << len(vid_masks) == vid_count and head_count % 2 == 0
    assert queries.shape[0] == 1 and queries.shape[3] == 1

    stays = working(lax.axis_index("tok"), tok_count)
    core = lax.axis_index("head") % 2
    flat = lambda array: array.reshape(groups, count, dim)
    q_all, k_all, v_all, c_all = (flat(a) for a in (queries, keys, values, out_grad))

    def gathered(arrays, after=None):
        own = jnp.stack(arrays).astype(F32)
        if after is not None:
            own, _ = lax.optimization_barrier((own, after))
        moved = swap_heads(own, tok_count, head_count)
        mine = jnp.where(stays, own, moved)
        return mine, flip(mine, "head", 1), moved

    top = groups - 1
    tokens = {}
    tokens[top] = gathered([q_all[top], c_all[top]])
    last = tokens[top][2]
    for index in reversed(range(top)):
        arrays = [q_all[index], c_all[index], k_all[index], v_all[index]]
        tokens[index] = gathered(arrays, last)
        last = tokens[index][2]

    init = fast_init.reshape(3, dim, dim)
    steps = updates.reshape(groups - 1, 3, dim, dim)
    vec_rows = 12
    pay_rows = groups * rows + (groups - 1) * vec_rows
    pad_rows = -pay_rows % 8
    full, mine, send = call(
        prep_kernel,
        [shape(groups - 1, 3, dim, dim)] + [shape(pay_rows + pad_rows, half)] * 2,
        init,
        steps,
    )
    weights = jnp.where(stays, mine, flip(send, "head", 1))
    level = lambda index: weights[index * rows : (index + 1) * rows]
    vectors = lambda index: weights[groups * rows + index * vec_rows :][:vec_rows]

    (query_grad,) = call(
        query_kernel,
        [shape(groups, count, dim, dtype=BF16)],
        q_all,
        c_all,
        init,
        full,
        flops=2 * groups * 10 * count * dim * dim,
    )

    n_parts = 2
    size = rows // n_parts
    part_shapes = [shape(size, half)] * n_parts
    sums_shape = shape(PAD, half)

    def reduced(outs):
        parts, sums = list(outs[:n_parts]), outs[n_parts]
        sums = sums + flip(sums, "head", 1)
        parts[0] = jnp.concatenate([parts[0], sums], axis=0)
        count_steps = len(tok_masks)
        for at in range(count_steps):
            moved = [
                flip(part, "tok", tok_masks[(at + j) % count_steps]) for j, part in enumerate(parts)
            ]
            if at + 1 < count_steps:
                parts = [part + other for part, other in zip(parts, moved)]
        return parts, moved

    product = 2 * 2 * count * dim * half
    outs = call(
        last_kernel,
        part_shapes + [sums_shape],
        tokens[top][0],
        tokens[top][1],
        level(top),
        flops=2 * 6 * product,
    )
    token_grads = {}
    for index in reversed(range(top)):
        own, other, _ = tokens[index]
        grad, coef = call(
            pre_kernel,
            [shape(rows, half), shape(7, 2 * count, half)],
            own,
            other,
            level(index),
            flops=2 * 9 * product,
        )
        parts, moved = reduced(outs)
        *outs, upper, mid = call(
            functools.partial(key_kernel, scale, share, n_parts),
            part_shapes + [sums_shape, shape(rows, half), shape(3, 2 * count, half)],
            *parts,
            *moved,
            own,
            other,
            level(index + 1),
            level(index),
            vectors(index),
            grad,
            coef,
            flops=2 * 6 * product,
        )
        d_mine, d_sib = call(
            token_kernel,
            [shape(2, count, dim)] * 2,
            mid,
            coef,
            level(index),
            upper,
            flops=3 * 6 * product,
        )
        d_mine = d_mine + flip(d_sib, "head", 1)
        token_grads[index] = (d_mine, swap_heads(d_mine, tok_count, head_count))

    dims = [("tok", mask) for mask in tok_masks] + [("vid", mask) for mask in vid_masks]
    orders = [dims[j % len(dims) :] + dims[: j % len(dims)] for j in range(3)]
    whole = jnp.concatenate(outs[:n_parts], axis=0)
    pieces = [whole[j * dim : (j + 1) * dim] for j in range(3)]
    for at in range(len(dims)):
        kept, sent = [], []
        for j in range(3):
            bit = bit_of(*orders[j][at])
            low, high = jnp.split(pieces[j], 2, axis=0)
            kept.append(jnp.where(bit, high, low))
            sent.append(jnp.where(bit, low, high))
        pieces = [kept[j] + flip(sent[j], *orders[j][at]) for j in range(3)]
    mine = jnp.stack(pieces)
    other = flip(mine, "head", 1)
    pair = jnp.stack([jnp.where(core == 0, mine, other), jnp.where(core == 0, other, mine)], axis=1)
    pair = jnp.where(stays, pair, share_heads(pair, tok_count, head_count))
    pieces = [pair[j] for j in range(3)]
    for at in reversed(range(len(dims))):
        moved = [flip(pieces[j], *orders[j][at]) for j in range(3)]
        if at == 0:
            break
        for j in range(3):
            bit = bit_of(*orders[j][at])
            low = jnp.where(bit, moved[j], pieces[j])
            high = jnp.where(bit, pieces[j], moved[j])
            pieces[j] = jnp.concatenate([low, high], axis=1)
    (init_grad,) = call(
        functools.partial(init_out_kernel, [orders[j][0] for j in range(3)]),
        [shape(3, dim, dim)],
        *[array for j in range(3) for array in (pieces[j], moved[j])],
    )

    key_grad, value_grad = call(
        functools.partial(tokens_out_kernel, tok_count),
        [shape(groups, count, dim, dtype=BF16)] * 2,
        *[array for index in range(top) for array in token_grads[index]],
    )
    back = lambda array: array.reshape(queries.shape)
    return back(query_grad), back(key_grad), back(value_grad), init_grad.reshape(fast_init.shape)


def solution(mesh):
    tokens = P("vid", None, "tok", "head", None)
    return jax.shard_map(
        on_device,
        mesh=mesh,
        in_specs=(
            tokens,
            tokens,
            tokens,
            tokens,
            P("head", None, None, None),
            P("vid", None, "head", None, None, None),
        ),
        out_specs=(tokens, tokens, tokens, P("head", None, None, None)),
        check_vma=False,
    )
```

```python
import functools

import jax
import jax.numpy as jnp
from jax import lax
from jax.experimental import pallas as pl
from jax.experimental.pallas import tpu as pltpu
from jax.sharding import PartitionSpec as P

EPS = 1e-06
F32 = jnp.float32
BF16 = jnp.bfloat16
NN = (((1,), (0,)), ((), ()))
NT = (((1,), (1,)), ((), ()))
TN = (((0,), (0,)), ((), ()))
PAD = 8
VEC = 12


def dot(left, right, dims):
    return lax.dot_general(left, right, dims, preferred_element_type=F32)


def split(array):
    high = array.astype(BF16)
    return high, (array - high.astype(F32)).astype(BF16)


def exact_left(left, right, dims):
    return dot(left, right[0], dims) + dot(left, right[1], dims)


def exact_right(left, right, dims):
    return dot(left[0], right, dims) + dot(left[1], right, dims)


def both_split(left, right, dims):
    return (
        dot(left[0], right[0], dims)
        + (dot(left[0], right[1], dims) + dot(left[1], right[0], dims))
    )


def silu_parts(gate):
    sigma = jax.nn.sigmoid(gate)
    rest = 1.0 - sigma
    silu = gate * sigma
    first = sigma * (1.0 + gate * rest)
    second = sigma * rest * (2.0 + gate * (1.0 - 2.0 * sigma))
    return silu, first, second


def rows_of_half(gate, up, down, which):
    dim = gate.shape[0]
    half = dim // 2
    cut = slice(which * half, (which + 1) * half)
    return [
        (0, gate[:, cut]),
        (dim, up[:, cut]),
        (2 * dim, down[cut, :half]),
        (2 * dim + half, down[cut, half:]),
    ]


def load_half(rows, dim):
    half = dim // 2
    gate_up = jnp.concatenate([rows[:dim], rows[dim : 2 * dim]], axis=1)
    down = jnp.concatenate([rows[2 * dim : 2 * dim + half], rows[2 * dim + half :]], axis=1)
    return gate_up, down


def prep_kernel(init_hbm, upd_hbm, full_ref, *refs):
    *halves, init_ref, upd_ref, sems = refs
    levels = range(upd_ref.shape[0])
    pairs = [(init_hbm, init_ref)] + [(upd_hbm.at[at], upd_ref.at[at]) for at in levels]
    fetch(pairs, sems)
    groups = upd_ref.shape[0] + 1
    dim = init_ref.shape[-1]
    half = dim // 2
    core = lax.axis_index("head") % 2
    weights = [init_ref[index].astype(F32) for index in range(3)]
    vectors = []
    levels = []
    for level in range(groups):
        levels.append(weights)
        if level + 1 == groups:
            break
        raised, ratio, cross, inverse = [], [], [], []
        for index in range(3):
            up = weights[index] + upd_ref[level, index].astype(F32)
            old2 = jnp.sum(weights[index] * weights[index], axis=0, keepdims=True) + EPS
            new2 = jnp.sum(up * up, axis=0, keepdims=True) + EPS
            old, new = jnp.sqrt(old2), jnp.sqrt(new2)
            ratio.append(old / new)
            cross.append(1.0 / (old * new))
            inverse.append(1.0 / old2)
            raised.append(up * ratio[index])
        vectors.append((ratio, cross, inverse))
        weights = raised
        for index in range(3):
            full_ref[level, index] = weights[index]

    def write(top_ref, ref, which):
        cut = slice(which * half, (which + 1) * half)
        for level in range(groups):
            target, base = (ref, level * 3 * dim) if level + 1 < groups else (top_ref, 0)
            for row, value in rows_of_half(*levels[level], which):
                target[base + row : base + row + value.shape[0], :] = value
        base = (groups - 1) * 3 * dim
        for kinds in vectors:
            for gate, up, down in kinds:
                for value in (gate[:, cut], up[:, cut], down[:, :half], down[:, half:]):
                    ref[base : base + 1, :] = value
                    base += 1

    @pl.when(core == 0)
    def _():
        write(*halves[:2], 0)
        write(*halves[2:], 1)

    @pl.when(core != 0)
    def _():
        write(*halves[:2], 1)
        write(*halves[2:], 0)


def query_kernel(q_ref, c_ref, init_ref, full_ref, out_ref):
    groups = q_ref.shape[0]
    for index in range(groups):
        query, cot = q_ref[index], c_ref[index]
        if index == 0:
            pieces = [(init_ref[part], None) for part in range(3)]
        else:
            pieces = [split(full_ref[index - 1, part]) for part in range(3)]

        def apply(left, right, dims):
            return dot(left, right[0], dims) if right[1] is None else exact_left(left, right, dims)

        gate = apply(query, pieces[0], NN)
        up = apply(query, pieces[1], NN)
        back = apply(cot, pieces[2], NT)
        silu, first, _ = silu_parts(gate)
        total = None
        for value, piece in ((back * up * first, pieces[0]), (back * silu, pieces[1])):
            value = split(value)
            term = exact_right(value, piece[0], NT) if piece[1] is None else both_split(value, piece, NT)
            total = term if total is None else total + term
        out_ref[index] = total.astype(out_ref.dtype)


def apply_terms(query, cot, rows, dim):
    half = dim // 2
    gate_up, down = load_half(rows, dim)
    raw = exact_left(query, split(gate_up), NN)
    back = exact_left(cot, split(down), NT)
    gate, up = raw[:, :half], raw[:, half:]
    silu, first, _ = silu_parts(gate)
    grads = jnp.concatenate([back * up * first, back * silu], axis=1)
    d_gate_up = exact_left(query, split(grads), TN)
    d_down = exact_right(split(silu * up), cot, TN)
    return d_gate_up, d_down


def fetch(pairs, sems):
    copies = [
        pltpu.make_async_copy(source, target, sems.at[at])
        for at, (source, target) in enumerate(pairs)
    ]
    for copy in copies:
        copy.start()
    for copy in copies:
        copy.wait()


def send_kernel(group, count, *refs):
    ins, outs, (scratch, sems) = refs[:count], refs[count:-2], refs[-2:]
    fetch([(ref.at[group], scratch.at[at]) for at, ref in enumerate(ins)], sems)
    for index in range(count):
        outs[index // 2][index % 2] = scratch[index].astype(F32)


def weights_kernel(tok_count, *refs):
    mine_ref, recv_ref = refs[:2]
    outs = refs[2:]
    stays = working(tok_count)

    def put(source):
        base = 0
        for ref in outs:
            ref[...] = source[base : base + ref.shape[0], :]
            base += ref.shape[0]

    pl.when(stays)(functools.partial(put, mine_ref))
    pl.when(jnp.logical_not(stays))(functools.partial(put, recv_ref))


def pick_tokens(tok_count, token_refs, scratch):
    count = token_refs[0].shape[1]
    stays = working(tok_count)

    def put(base, first, second):
        for index in range(2):
            scratch[base + index, :count, :] = first[index].astype(BF16)
            scratch[base + index, count:, :] = second[index].astype(BF16)

    for base in range(0, scratch.shape[0], 2):
        own_ref, first_ref, late_ref = token_refs[3 * base // 2 :][:3]
        pl.when(stays)(functools.partial(put, base, own_ref, first_ref))
        pl.when(jnp.logical_not(stays))(functools.partial(put, base, first_ref, late_ref))


def last_kernel(tok_count, *refs):
    token_refs, w_ref, out_ref, scratch = refs[:3], *refs[3:]
    dim = scratch.shape[-1]
    half = dim // 2
    pick_tokens(tok_count, token_refs, scratch)
    d_gate_up, d_down = apply_terms(scratch[0], scratch[1], w_ref[...], dim)
    out_ref[:dim, :] = d_gate_up[:, :half]
    out_ref[dim : 2 * dim, :] = d_gate_up[:, half:]
    out_ref[3 * dim :, :] = jnp.zeros((PAD, half), F32)
    for block in range(2):
        value = d_down[:, block * half : (block + 1) * half]
        row = 2 * dim + block * half
        out_ref[row : row + half, :] = value
        out_ref[3 * dim + block : 3 * dim + block + 1, :] = jnp.sum(
            value * w_ref[row : row + half, :], axis=0, keepdims=True
        )


def pre_kernel(tok_count, *refs):
    token_refs, w_ref, grad_ref, coef_ref, tok_ref, scratch = refs[:6], *refs[6:]
    dim = scratch.shape[-1]
    half = dim // 2
    pick_tokens(tok_count, token_refs, scratch)
    query, cot, key, value = (scratch[index] for index in range(4))
    tok_ref[0] = key
    tok_ref[1] = value
    rows = w_ref[...]
    d_gate_up, d_down = apply_terms(query, cot, rows, dim)
    grad_ref[:dim, :] = d_gate_up[:, :half]
    grad_ref[dim : 2 * dim, :] = d_gate_up[:, half:]
    grad_ref[2 * dim : 2 * dim + half, :] = d_down[:, :half]
    grad_ref[2 * dim + half :, :] = d_down[:, half:]
    gate_up, down = load_half(rows, dim)
    raw = exact_left(key, split(gate_up), NN)
    back = exact_left(value, split(down), NT)
    gate, up = raw[:, :half], raw[:, half:]
    silu, first, second = silu_parts(gate)
    coef_ref[0] = first * up
    coef_ref[1] = silu
    coef_ref[2] = back * second * up
    coef_ref[3] = back * first
    coef_ref[4] = back * first * up
    coef_ref[5] = back * silu
    coef_ref[6] = silu * up


def add_kernel(mine_ref, recv_ref, out_ref, *tail_refs):
    total = mine_ref[...] + recv_ref[...]
    out_ref[...] = total
    for ref in tail_refs:
        ref[...] = total[total.shape[0] - ref.shape[0] :]


def key_kernel(scale, share, order, *refs):
    total_ref, sums_ref, sib_ref, tok_ref, new_ref, old_ref, vec_ref, grad_ref, coef_ref = refs[:9]
    *outs, up_ref, mid_ref = refs[9:]
    dim = tok_ref.shape[-1]
    half = dim // 2
    down_sums = sums_ref[...] + sib_ref[...]
    pieces = ((0, dim, 0), (dim, dim, 1), (2 * dim, half, 2), (2 * dim + half, half, 3))
    upper, carried = [], []
    for row, rows, slot in pieces:
        adj = total_ref[row : row + rows, :]
        new = new_ref[row : row + rows, :]
        if slot < 2:
            sums = jnp.sum(new * adj, axis=0, keepdims=True)
        else:
            sums = down_sums[slot - 2 : slot - 1]
        ratio = vec_ref[slot : slot + 1, :]
        cross = vec_ref[4 + slot : 5 + slot, :]
        inverse = vec_ref[8 + slot : 9 + slot, :]
        up_adj = adj * ratio - new * (sums * cross)
        direct = old_ref[row : row + rows, :] * (sums * inverse)
        upper.append(up_adj * scale)
        carried.append((up_adj + direct) * share + grad_ref[row : row + rows, :])
        up_ref[row : row + rows, :] = upper[-1]
    key, value = tok_ref[0], tok_ref[1]
    raw = exact_left(key, split(jnp.concatenate(upper[:2], axis=1)), NN)
    back = exact_left(value, split(jnp.concatenate(upper[2:], axis=1)), NT)
    gate, up = raw[:, :half], raw[:, half:]
    hidden = coef_ref[0] * gate + coef_ref[1] * up
    d_gate = coef_ref[2] * gate + coef_ref[3] * up + coef_ref[0] * back
    d_up = coef_ref[3] * gate + coef_ref[1] * back
    d_gate_up = exact_left(key, split(jnp.concatenate([d_gate, d_up], axis=1)), TN)
    d_down = exact_right(split(hidden), value, TN)
    mid_ref[0] = d_gate
    mid_ref[1] = d_up
    mid_ref[2] = hidden
    results = [
        d_gate_up[:, :half] + carried[0],
        d_gate_up[:, half:] + carried[1],
        d_down[:, :half] + carried[2],
        d_down[:, half:] + carried[3],
    ]
    if order is None:
        (out_ref,) = outs
        out_ref[3 * dim :, :] = jnp.zeros((PAD, half), F32)
        for (row, rows, slot), value in zip(pieces, results):
            out_ref[row : row + rows, :] = value
            if slot >= 2:
                out_ref[3 * dim + slot - 2 : 3 * dim + slot - 1, :] = jnp.sum(
                    value * old_ref[row : row + rows, :], axis=0, keepdims=True
                )
    else:
        halves = [[results[0][:half], results[1][:half], results[2]]]
        halves.append([results[0][half:], results[1][half:], results[3]])
        store_halves(halves, order, *outs)


def store_halves(halves, order, keep_ref, send_ref):
    bit = bit_of(order)

    def put(kept, sent):
        for index in range(3):
            keep_ref[index] = kept[index]
            send_ref[index] = sent[index]

    pl.when(bit)(functools.partial(put, halves[1], halves[0]))
    pl.when(jnp.logical_not(bit))(functools.partial(put, halves[0], halves[1]))


def halve_kernel(order, mine_ref, recv_ref, *outs):
    total = mine_ref[...] + recv_ref[...]
    if order is None:
        outs[0][...] = total
        return
    size = total.shape[1] // 2
    halves = [[total[m, at * size : (at + 1) * size] for m in range(3)] for at in range(2)]
    store_halves(halves, order, *outs)


def pair_kernel(mine_ref, other_ref, out_ref):
    out_ref[0] = mine_ref[...]
    out_ref[1] = other_ref[...]


def choose_kernel(tok_count, own_ref, moved_ref, out_ref):
    stays = working(tok_count)

    def put(source):
        out_ref[...] = source[...]

    pl.when(stays)(functools.partial(put, own_ref))
    pl.when(jnp.logical_not(stays))(functools.partial(put, moved_ref))


def init_out_kernel(tok_count, rs_orders, ag_orders, mine_ref, recv_ref, out_ref):
    dim = out_ref.shape[-1]
    half = dim // 2
    blocks = mine_ref.shape[0]
    size = mine_ref.shape[3]
    steps = len(ag_orders[0])
    stays = working(tok_count)
    for core in range(2):

        @pl.when(lax.axis_index("head") % 2 == core)
        def _():
            for flipped in range(2 * blocks):
                source = mine_ref if flipped < blocks else recv_ref
                where = flipped % blocks
                for slot in range(2):
                    which = core if slot == 0 else 1 - core
                    offset, first = 0, None
                    for at, (axis, mask) in enumerate(rs_orders[which]):
                        bit = (lax.axis_index(axis) // mask) % 2
                        step = ag_orders[core].index((axis, mask))
                        if (flipped >> step) & 1:
                            bit = 1 - bit
                        if at == 0:
                            first = bit
                        else:
                            offset = offset + bit * (dim >> (at + 1))
                    offset = pl.multiple_of(offset, size)
                    low = first * half + offset
                    for index in range(2):
                        out_ref[index, pl.ds(pl.multiple_of(low, size), size), which * half : (which + 1) * half] = (
                            source[where, slot, index]
                        )
                    rows = pl.ds(pl.multiple_of(which * half + offset, size), size)
                    pl.when(first == 0)(functools.partial(put_block, out_ref, rows, slice(0, half), source, where, slot))
                    pl.when(first == 1)(functools.partial(put_block, out_ref, rows, slice(half, dim), source, where, slot))


def put_block(out_ref, rows, lanes, source, where, slot):
    out_ref[2, rows, lanes] = source[where, slot, 2]


def token_kernel(tok_count, mid_ref, coef_ref, w_ref, up_ref, keep_ref, give_ref):
    dim = keep_ref.shape[-1]
    count = keep_ref.shape[1]
    w_gate_up, w_down = load_half(w_ref[...], dim)
    u_gate_up, u_down = load_half(up_ref[...], dim)
    left = jnp.concatenate([mid_ref[0], mid_ref[1]], axis=1)
    d_key = both_split(split(left), split(w_gate_up), NT)
    left = jnp.concatenate([coef_ref[4], coef_ref[5]], axis=1)
    d_key = d_key + both_split(split(left), split(u_gate_up), NT)
    left = jnp.concatenate([mid_ref[2], coef_ref[6]], axis=1)
    right = jnp.concatenate([w_down, u_down], axis=0)
    d_value = both_split(split(left), split(right), NN)

    def put(first, second):
        for index, value in enumerate((d_key, d_value)):
            first[index] = value[:count]
            second[index] = value[count:]

    stays = working(tok_count)
    pl.when(stays)(functools.partial(put, keep_ref, give_ref))
    pl.when(jnp.logical_not(stays))(functools.partial(put, give_ref, keep_ref))


def tokens_out_kernel(tok_count, *refs):
    key_ref, value_ref = refs[-2:]
    stays = working(tok_count)
    ins = refs[:-2]
    groups = len(ins) // 2
    for index in range(groups):

        def put(source):
            key_ref[index] = source[0].astype(key_ref.dtype)
            value_ref[index] = source[1].astype(value_ref.dtype)

        pl.when(stays)(functools.partial(put, ins[2 * index]))
        pl.when(jnp.logical_not(stays))(functools.partial(put, ins[2 * index + 1]))
    key_ref[groups] = jnp.zeros_like(key_ref[groups])
    value_ref[groups] = jnp.zeros_like(value_ref[groups])


def call(kernel, outs, *args, scratch=(), limit=16, **kwargs):
    return pl.pallas_call(
        kernel,
        out_shape=outs,
        **kwargs,
        scratch_shapes=scratch,
        cost_estimate=pl.CostEstimate(flops=1, bytes_accessed=1, transcendentals=0),
        compiler_params=pltpu.CompilerParams(vmem_limit_bytes=limit * 1024 * 1024),
    )(*args)


def shape(*dims, dtype=F32):
    return jax.ShapeDtypeStruct(dims, dtype)


def tie(array, after):
    return lax.optimization_barrier((array, after))[0]


def working(tok_count):
    return lax.axis_index("tok") // (tok_count // 2) == lax.axis_index("head") % 2


def bit_of(order):
    bits = [(lax.axis_index(axis) // mask) % 2 for axis, mask in order]
    return jnp.where(lax.axis_index("head") % 2 == 0, bits[0], bits[1]) == 1


def on_device(queries, keys, values, out_grad, fast_init, updates):
    tok_count = lax.axis_size("tok")
    head_count = lax.axis_size("head")
    vid_count = lax.axis_size("vid")
    _, groups, count, _, dim = queries.shape
    half = dim // 2
    rows = 3 * dim
    scale = float(count * tok_count) ** (-0.5)
    share = 2.0 / tok_count
    tok_dims = [("tok", 1 << i) for i in range((tok_count // 2).bit_length() - 1)]
    vid_dims = [("vid", 1 << i) for i in range(vid_count.bit_length() - 1)]
    assert len(tok_dims) >= 1 and 2 << len(tok_dims) == tok_count
    assert 1 << len(vid_dims) == vid_count and head_count % 2 == 0
    assert queries.shape[0] == 1 and queries.shape[3] == 1

    def stays_at(tok, head):
        return tok // (tok_count // 2) == head % 2

    def permute(array, goes):
        pairs = []
        for tok in range(tok_count):
            for head in range(head_count):
                for vid in range(vid_count):
                    there = goes(tok, head, vid)
                    if there is not None:
                        number = lambda t, h, v: (t * head_count + h) * vid_count + v
                        pairs.append((number(tok, head, vid), number(*there)))
        return lax.ppermute(array, ("tok", "head", "vid"), pairs)

    def meet(array, order):
        def goes(tok, head, vid):
            axis, mask = order[head % 2]
            return (tok ^ mask, head, vid) if axis == "tok" else (tok, head, vid ^ mask)

        return permute(array, goes)

    def sibling(array, from_staying=None):
        def goes(tok, head, vid):
            if from_staying is None or stays_at(tok, head) == from_staying:
                return (tok, head ^ 1, vid)

        return permute(array, goes)

    def spread(array):
        def goes(tok, head, vid):
            if stays_at(tok, head):
                return (tok, head ^ 1, vid)
            return (tok ^ (tok_count // 2), head, vid)

        return permute(array, goes)

    def swap(array):
        def goes(tok, head, vid):
            if not stays_at(tok, head):
                return (tok ^ (tok_count // 2), head ^ 1, vid)

        return permute(array, goes)

    def lend(array):
        def goes(tok, head, vid):
            if stays_at(tok, head):
                return (tok ^ (tok_count // 2), head, vid)

        return permute(array, goes)

    flat = lambda array: array.reshape(groups, count, dim)
    q_all, k_all, v_all, c_all = (flat(a) for a in (queries, keys, values, out_grad))
    top = groups - 1
    init = fast_init.reshape(3, dim, dim)
    steps = updates.reshape(groups - 1, 3, dim, dim)

    def send(arrays, index, limit=16):
        return call(
            functools.partial(send_kernel, index, len(arrays)),
            [shape(2, count, dim)] * (len(arrays) // 2),
            *arrays,
            limit=limit,
            in_specs=[pl.BlockSpec(memory_space=pltpu.HBM)] * len(arrays),
            scratch=[
                pltpu.VMEM((len(arrays), count, dim), BF16),
                pltpu.SemaphoreType.DMA((len(arrays),)),
            ],
        )

    own = {top: send([q_all, c_all], top, 60)}
    first = {top: [spread(own[top][0])]}
    init = tie(init, own[top][0])

    low_rows = top * rows + top * VEC
    low_rows += -low_rows % 8
    full, *halves = call(
        prep_kernel,
        [shape(top, 3, dim, dim)] + [shape(rows, half), shape(low_rows, half)] * 2,
        init,
        steps,
        in_specs=[pl.BlockSpec(memory_space=pltpu.HBM)] * 2,
        scratch=[
            pltpu.VMEM(init.shape, BF16),
            pltpu.VMEM(steps.shape, BF16),
            pltpu.SemaphoreType.DMA((groups,)),
        ],
    )

    def chosen(outs, mine, sent):
        return call(functools.partial(weights_kernel, tok_count), outs, mine, sibling(sent))

    (top_weights,) = chosen([shape(rows, half)], halves[0], halves[2])
    (query_grad,) = call(query_kernel, [shape(groups, count, dim, dtype=BF16)], q_all, c_all, init, full)

    def tokens(index, after):
        arrays = []
        for mine, arrived in zip(own[index], first[index]):
            arrays += [mine, arrived, sibling(tie(arrived, after), True)]
        return arrays

    def scratch(index):
        return [pltpu.VMEM((2 * len(own[index]), 2 * count, dim), BF16)]

    both = 2 * count
    (payload,) = call(
        functools.partial(last_kernel, tok_count),
        [shape(rows + PAD, half)],
        *tokens(top, query_grad),
        top_weights,
        scratch=scratch(top),
    )
    weights = chosen(
        [shape(rows, half)] * top + [shape(VEC, half)] * top, halves[1], tie(halves[3], first[top][0])
    )
    factors = list(weights[top:])
    weights = [*weights[:top], top_weights]
    token_grads = {}
    for index in reversed(range(top)):
        own[index] = send([q_all, c_all, k_all, v_all], index)
        first[index] = [spread(tie(array, first[index + 1])) for array in own[index]]
        for at in range(len(tok_dims)):
            arrived = meet(payload, (tok_dims[at], tok_dims[at - 1]))
            if at + 1 < len(tok_dims):
                (payload,) = call(add_kernel, [shape(rows + PAD, half)], payload, arrived)
        grad, coef, keyed = call(
            functools.partial(pre_kernel, tok_count),
            [shape(rows, half), shape(7, both, half), shape(2, both, dim, dtype=BF16)],
            *tokens(index, payload),
            weights[index],
            scratch=scratch(index),
        )
        total, sums = call(add_kernel, [shape(rows + PAD, half), shape(PAD, half)], payload, arrived)
        if index > 0:
            out_shapes, order = [shape(rows + PAD, half)], None
        else:
            dims = tok_dims[:1] + vid_dims + tok_dims[1:]
            rs_orders = [dims, dims[-1:] + dims[:-1]]
            order = [rs_orders[0][0], rs_orders[1][0]]
            out_shapes = [shape(3, half, half)] * 2
        *outs, upper, mid = call(
            functools.partial(key_kernel, scale, share, order),
            out_shapes + [shape(rows, half), shape(3, both, half)],
            total,
            sums,
            sibling(sums),
            keyed,
            weights[index + 1],
            weights[index],
            factors[index],
            grad,
            coef,
        )
        payload = outs[0]
        keep, give = call(
            functools.partial(token_kernel, tok_count),
            [shape(2, count, dim)] * 2,
            mid,
            coef,
            weights[index],
            upper,
        )
        (d_tokens,) = call(add_kernel, [shape(2, count, dim)], keep, sibling(give))
        token_grads[index] = d_tokens

    kept, sends = outs
    for at in range(len(dims)):
        arrived = meet(sends, [order[at] for order in rs_orders])
        if at + 1 < len(dims):
            out_shapes = [shape(3, kept.shape[1] // 2, half)] * 2
            order = [order[at + 1] for order in rs_orders]
            kept, sends = call(functools.partial(halve_kernel, order), out_shapes, kept, arrived)
        else:
            (kept,) = call(functools.partial(halve_kernel, None), [shape(*kept.shape)], kept, arrived)
    (pair,) = call(pair_kernel, [shape(2, *kept.shape)], kept, sibling(kept))
    (block,) = call(
        functools.partial(choose_kernel, tok_count), [shape(*pair.shape)], pair, lend(pair)
    )
    block = block[None]
    ag_orders = [order[::-1] for order in rs_orders]
    for at in range(len(dims)):
        arrived = meet(block, [order[at] for order in ag_orders])
        if at + 1 < len(dims):
            (pair,) = call(pair_kernel, [shape(2, *block.shape)], block, arrived)
            block = pair.reshape(2 * block.shape[0], *block.shape[1:])
    (init_grad,) = call(
        functools.partial(init_out_kernel, tok_count, rs_orders, ag_orders),
        [shape(3, dim, dim)],
        block,
        arrived,
    )
    arrays = []
    for index in range(top):
        arrays += [token_grads[index], swap(token_grads[index])]
    key_grad, value_grad = call(
        functools.partial(tokens_out_kernel, tok_count),
        [shape(groups, count, dim, dtype=BF16)] * 2,
        *arrays,
    )
    back = lambda array: array.reshape(queries.shape)
    return back(query_grad), back(key_grad), back(value_grad), init_grad.reshape(fast_init.shape)


def solution(mesh):
    tokens = P("vid", None, "tok", "head", None)
    return jax.shard_map(
        on_device,
        mesh=mesh,
        in_specs=(
            tokens,
            tokens,
            tokens,
            tokens,
            P("head", None, None, None),
            P("vid", None, "head", None, None, None),
        ),
        out_specs=(tokens, tokens, tokens, P("head", None, None, None)),
        check_vma=False,
    )
```

```python
import functools

import jax
import jax.numpy as jnp
from jax import lax
from jax.experimental import pallas as pl
from jax.experimental.pallas import tpu as pltpu
from jax.sharding import PartitionSpec as P

EPS = 1e-06
F32 = jnp.float32
BF16 = jnp.bfloat16
NN = (((1,), (0,)), ((), ()))
NT = (((1,), (1,)), ((), ()))
TN = (((0,), (0,)), ((), ()))
PAD = 8
VEC = 12


def dot(left, right, dims):
    return lax.dot_general(left, right, dims, preferred_element_type=F32)


def split(array):
    high = array.astype(BF16)
    return high, (array - high.astype(F32)).astype(BF16)


def exact_left(left, right, dims):
    return dot(left, right[0], dims) + dot(left, right[1], dims)


def exact_right(left, right, dims):
    return dot(left[0], right, dims) + dot(left[1], right, dims)


def both_split(left, right, dims):
    return (
        dot(left[0], right[0], dims)
        + (dot(left[0], right[1], dims) + dot(left[1], right[0], dims))
    )


def silu_parts(gate):
    sigma = jax.nn.sigmoid(gate)
    rest = 1.0 - sigma
    silu = gate * sigma
    first = sigma * (1.0 + gate * rest)
    second = sigma * rest * (2.0 + gate * (1.0 - 2.0 * sigma))
    return silu, first, second


def rows_of_half(gate, up, down, which):
    dim = gate.shape[0]
    half = dim // 2
    cut = slice(which * half, (which + 1) * half)
    return [
        (0, gate[:, cut]),
        (dim, up[:, cut]),
        (2 * dim, down[cut, :half]),
        (2 * dim + half, down[cut, half:]),
    ]


def load_half(rows, dim):
    half = dim // 2
    gate_up = jnp.concatenate([rows[:dim], rows[dim : 2 * dim]], axis=1)
    down = jnp.concatenate([rows[2 * dim : 2 * dim + half], rows[2 * dim + half :]], axis=1)
    return gate_up, down


def prep_kernel(init_hbm, upd_hbm, full_ref, *refs):
    *halves, init_ref, upd_ref, sems = refs
    levels = range(upd_ref.shape[0])
    pairs = [(init_hbm, init_ref)] + [(upd_hbm.at[at], upd_ref.at[at]) for at in levels]
    fetch(pairs, sems)
    groups = upd_ref.shape[0] + 1
    dim = init_ref.shape[-1]
    half = dim // 2
    core = lax.axis_index("head") % 2
    weights = [init_ref[index].astype(F32) for index in range(3)]
    vectors = []
    levels = []
    for level in range(groups):
        levels.append(weights)
        if level + 1 == groups:
            break
        raised, ratio, cross, inverse = [], [], [], []
        for index in range(3):
            up = weights[index] + upd_ref[level, index].astype(F32)
            old2 = jnp.sum(weights[index] * weights[index], axis=0, keepdims=True) + EPS
            new2 = jnp.sum(up * up, axis=0, keepdims=True) + EPS
            old, new = jnp.sqrt(old2), jnp.sqrt(new2)
            ratio.append(old / new)
            cross.append(1.0 / (old * new))
            inverse.append(1.0 / old2)
            raised.append(up * ratio[index])
        vectors.append((ratio, cross, inverse))
        weights = raised
        for index in range(3):
            full_ref[level, index] = weights[index]

    def write(top_ref, ref, which):
        cut = slice(which * half, (which + 1) * half)
        for level in range(groups):
            target, base = (ref, level * 3 * dim) if level + 1 < groups else (top_ref, 0)
            for row, value in rows_of_half(*levels[level], which):
                target[base + row : base + row + value.shape[0], :] = value
        base = (groups - 1) * 3 * dim
        for kinds in vectors:
            for gate, up, down in kinds:
                for value in (gate[:, cut], up[:, cut], down[:, :half], down[:, half:]):
                    ref[base : base + 1, :] = value
                    base += 1

    @pl.when(core == 0)
    def _():
        write(*halves[:2], 0)
        write(*halves[2:], 1)

    @pl.when(core != 0)
    def _():
        write(*halves[:2], 1)
        write(*halves[2:], 0)


def query_kernel(q_ref, c_ref, init_ref, full_ref, out_ref):
    groups = q_ref.shape[0]
    for index in range(groups):
        query, cot = q_ref[index], c_ref[index]
        if index == 0:
            pieces = [(init_ref[part], None) for part in range(3)]
        else:
            pieces = [split(full_ref[index - 1, part]) for part in range(3)]

        def apply(left, right, dims):
            return dot(left, right[0], dims) if right[1] is None else exact_left(left, right, dims)

        gate = apply(query, pieces[0], NN)
        up = apply(query, pieces[1], NN)
        back = apply(cot, pieces[2], NT)
        silu, first, _ = silu_parts(gate)
        total = None
        for value, piece in ((back * up * first, pieces[0]), (back * silu, pieces[1])):
            value = split(value)
            term = exact_right(value, piece[0], NT) if piece[1] is None else both_split(value, piece, NT)
            total = term if total is None else total + term
        out_ref[index] = total.astype(out_ref.dtype)


def apply_terms(query, cot, rows, dim):
    half = dim // 2
    gate_up, down = load_half(rows, dim)
    raw = exact_left(query, split(gate_up), NN)
    back = exact_left(cot, split(down), NT)
    gate, up = raw[:, :half], raw[:, half:]
    silu, first, _ = silu_parts(gate)
    grads = jnp.concatenate([back * up * first, back * silu], axis=1)
    d_gate_up = exact_left(query, split(grads), TN)
    d_down = exact_right(split(silu * up), cot, TN)
    return d_gate_up, d_down


def fetch(pairs, sems):
    copies = [
        pltpu.make_async_copy(source, target, sems.at[at])
        for at, (source, target) in enumerate(pairs)
    ]
    for copy in copies:
        copy.start()
    for copy in copies:
        copy.wait()


def send_kernel(group, count, *refs):
    ins, outs, (scratch, sems) = refs[:count], refs[count:-2], refs[-2:]
    fetch([(ref.at[group], scratch.at[at]) for at, ref in enumerate(ins)], sems)
    for index in range(count):
        outs[index // 2][index % 2] = scratch[index].astype(F32)


def weights_kernel(tok_count, *refs):
    mine_ref, recv_ref = refs[:2]
    outs = refs[2:]
    stays = working(tok_count)

    def put(source):
        base = 0
        for ref in outs:
            ref[...] = source[base : base + ref.shape[0], :]
            base += ref.shape[0]

    pl.when(stays)(functools.partial(put, mine_ref))
    pl.when(jnp.logical_not(stays))(functools.partial(put, recv_ref))


def pick_tokens(tok_count, token_refs, scratch):
    count = token_refs[0].shape[1]
    stays = working(tok_count)

    def put(base, first, second):
        for index in range(2):
            scratch[base + index, :count, :] = first[index].astype(BF16)
            scratch[base + index, count:, :] = second[index].astype(BF16)

    for base in range(0, scratch.shape[0], 2):
        own_ref, first_ref, late_ref = token_refs[3 * base // 2 :][:3]
        pl.when(stays)(functools.partial(put, base, own_ref, first_ref))
        pl.when(jnp.logical_not(stays))(functools.partial(put, base, first_ref, late_ref))


def last_kernel(tok_count, *refs):
    token_refs, w_ref, out_ref, scratch = refs[:3], *refs[3:]
    dim = scratch.shape[-1]
    half = dim // 2
    pick_tokens(tok_count, token_refs, scratch)
    d_gate_up, d_down = apply_terms(scratch[0], scratch[1], w_ref[...], dim)
    out_ref[:dim, :] = d_gate_up[:, :half]
    out_ref[dim : 2 * dim, :] = d_gate_up[:, half:]
    out_ref[3 * dim :, :] = jnp.zeros((PAD, half), F32)
    for block in range(2):
        value = d_down[:, block * half : (block + 1) * half]
        row = 2 * dim + block * half
        out_ref[row : row + half, :] = value
        out_ref[3 * dim + block : 3 * dim + block + 1, :] = jnp.sum(
            value * w_ref[row : row + half, :], axis=0, keepdims=True
        )


def pre_kernel(tok_count, *refs):
    token_refs, w_ref, grad_ref, coef_ref, tok_ref, scratch = refs[:6], *refs[6:]
    dim = scratch.shape[-1]
    half = dim // 2
    pick_tokens(tok_count, token_refs, scratch)
    query, cot, key, value = (scratch[index] for index in range(4))
    tok_ref[0] = key
    tok_ref[1] = value
    rows = w_ref[...]
    d_gate_up, d_down = apply_terms(query, cot, rows, dim)
    grad_ref[:dim, :] = d_gate_up[:, :half]
    grad_ref[dim : 2 * dim, :] = d_gate_up[:, half:]
    grad_ref[2 * dim : 2 * dim + half, :] = d_down[:, :half]
    grad_ref[2 * dim + half :, :] = d_down[:, half:]
    gate_up, down = load_half(rows, dim)
    raw = exact_left(key, split(gate_up), NN)
    back = exact_left(value, split(down), NT)
    gate, up = raw[:, :half], raw[:, half:]
    silu, first, second = silu_parts(gate)
    coef_ref[0] = first * up
    coef_ref[1] = silu
    coef_ref[2] = back * second * up
    coef_ref[3] = back * first
    coef_ref[4] = back * first * up
    coef_ref[5] = back * silu
    coef_ref[6] = silu * up


def add_kernel(mine_ref, recv_ref, out_ref, *tail_refs):
    total = mine_ref[...] + recv_ref[...]
    out_ref[...] = total
    for ref in tail_refs:
        ref[...] = total[total.shape[0] - ref.shape[0] :]


def key_kernel(scale, share, order, *refs):
    total_ref, sums_ref, sib_ref, tok_ref, new_ref, old_ref, vec_ref, grad_ref, coef_ref = refs[:9]
    *outs, up_ref, mid_ref = refs[9:]
    dim = tok_ref.shape[-1]
    half = dim // 2
    down_sums = sums_ref[...] + sib_ref[...]
    pieces = ((0, dim, 0), (dim, dim, 1), (2 * dim, half, 2), (2 * dim + half, half, 3))
    upper, carried = [], []
    for row, rows, slot in pieces:
        adj = total_ref[row : row + rows, :]
        new = new_ref[row : row + rows, :]
        if slot < 2:
            sums = jnp.sum(new * adj, axis=0, keepdims=True)
        else:
            sums = down_sums[slot - 2 : slot - 1]
        ratio = vec_ref[slot : slot + 1, :]
        cross = vec_ref[4 + slot : 5 + slot, :]
        inverse = vec_ref[8 + slot : 9 + slot, :]
        up_adj = adj * ratio - new * (sums * cross)
        direct = old_ref[row : row + rows, :] * (sums * inverse)
        upper.append(up_adj * scale)
        carried.append((up_adj + direct) * share + grad_ref[row : row + rows, :])
        up_ref[row : row + rows, :] = upper[-1]
    key, value = tok_ref[0], tok_ref[1]
    raw = exact_left(key, split(jnp.concatenate(upper[:2], axis=1)), NN)
    back = exact_left(value, split(jnp.concatenate(upper[2:], axis=1)), NT)
    gate, up = raw[:, :half], raw[:, half:]
    hidden = coef_ref[0] * gate + coef_ref[1] * up
    d_gate = coef_ref[2] * gate + coef_ref[3] * up + coef_ref[0] * back
    d_up = coef_ref[3] * gate + coef_ref[1] * back
    d_gate_up = exact_left(key, split(jnp.concatenate([d_gate, d_up], axis=1)), TN)
    d_down = exact_right(split(hidden), value, TN)
    mid_ref[0] = d_gate
    mid_ref[1] = d_up
    mid_ref[2] = hidden
    results = [
        d_gate_up[:, :half] + carried[0],
        d_gate_up[:, half:] + carried[1],
        d_down[:, :half] + carried[2],
        d_down[:, half:] + carried[3],
    ]
    if order is None:
        (out_ref,) = outs
        out_ref[3 * dim :, :] = jnp.zeros((PAD, half), F32)
        for (row, rows, slot), value in zip(pieces, results):
            out_ref[row : row + rows, :] = value
            if slot >= 2:
                out_ref[3 * dim + slot - 2 : 3 * dim + slot - 1, :] = jnp.sum(
                    value * old_ref[row : row + rows, :], axis=0, keepdims=True
                )
    else:
        halves = [[results[0][:half], results[1][:half], results[2]]]
        halves.append([results[0][half:], results[1][half:], results[3]])
        store_halves(halves, order, *outs)


def store_halves(halves, order, keep_ref, send_ref):
    bit = bit_of(order)

    def put(kept, sent):
        for index in range(3):
            keep_ref[index] = kept[index]
            send_ref[index] = sent[index]

    pl.when(bit)(functools.partial(put, halves[1], halves[0]))
    pl.when(jnp.logical_not(bit))(functools.partial(put, halves[0], halves[1]))


def halve_kernel(order, mine_ref, recv_ref, *outs):
    total = mine_ref[...] + recv_ref[...]
    if order is None:
        outs[0][...] = total
        return
    size = total.shape[1] // 2
    halves = [[total[m, at * size : (at + 1) * size] for m in range(3)] for at in range(2)]
    store_halves(halves, order, *outs)


def pair_kernel(mine_ref, other_ref, out_ref):
    out_ref[0] = mine_ref[...]
    out_ref[1] = other_ref[...]


def choose_kernel(tok_count, own_ref, moved_ref, out_ref):
    stays = working(tok_count)

    def put(source):
        out_ref[...] = source[...]

    pl.when(stays)(functools.partial(put, own_ref))
    pl.when(jnp.logical_not(stays))(functools.partial(put, moved_ref))


def init_out_kernel(tok_count, rs_orders, ag_orders, mine_ref, recv_ref, out_ref):
    dim = out_ref.shape[-1]
    half = dim // 2
    blocks = mine_ref.shape[0]
    size = mine_ref.shape[3]
    steps = len(ag_orders[0])
    stays = working(tok_count)
    for core in range(2):

        @pl.when(lax.axis_index("head") % 2 == core)
        def _():
            for flipped in range(2 * blocks):
                source = mine_ref if flipped < blocks else recv_ref
                where = flipped % blocks
                for slot in range(2):
                    which = core if slot == 0 else 1 - core
                    offset, first = 0, None
                    for at, (axis, mask) in enumerate(rs_orders[which]):
                        bit = (lax.axis_index(axis) // mask) % 2
                        step = ag_orders[core].index((axis, mask))
                        if (flipped >> step) & 1:
                            bit = 1 - bit
                        if at == 0:
                            first = bit
                        else:
                            offset = offset + bit * (dim >> (at + 1))
                    offset = pl.multiple_of(offset, size)
                    low = first * half + offset
                    for index in range(2):
                        out_ref[index, pl.ds(pl.multiple_of(low, size), size), which * half : (which + 1) * half] = (
                            source[where, slot, index]
                        )
                    rows = pl.ds(pl.multiple_of(which * half + offset, size), size)
                    pl.when(first == 0)(functools.partial(put_block, out_ref, rows, slice(0, half), source, where, slot))
                    pl.when(first == 1)(functools.partial(put_block, out_ref, rows, slice(half, dim), source, where, slot))


def put_block(out_ref, rows, lanes, source, where, slot):
    out_ref[2, rows, lanes] = source[where, slot, 2]


def token_kernel(tok_count, mid_ref, coef_ref, w_ref, up_ref, keep_ref, give_ref):
    dim = keep_ref.shape[-1]
    count = keep_ref.shape[1]
    w_gate_up, w_down = load_half(w_ref[...], dim)
    u_gate_up, u_down = load_half(up_ref[...], dim)
    left = jnp.concatenate([mid_ref[0], mid_ref[1]], axis=1)
    d_key = both_split(split(left), split(w_gate_up), NT)
    left = jnp.concatenate([coef_ref[4], coef_ref[5]], axis=1)
    d_key = d_key + both_split(split(left), split(u_gate_up), NT)
    left = jnp.concatenate([mid_ref[2], coef_ref[6]], axis=1)
    right = jnp.concatenate([w_down, u_down], axis=0)
    d_value = both_split(split(left), split(right), NN)

    def put(first, second):
        for index, value in enumerate((d_key, d_value)):
            first[index] = value[:count]
            second[index] = value[count:]

    stays = working(tok_count)
    pl.when(stays)(functools.partial(put, keep_ref, give_ref))
    pl.when(jnp.logical_not(stays))(functools.partial(put, give_ref, keep_ref))


def tokens_out_kernel(tok_count, *refs):
    key_ref, value_ref = refs[-2:]
    stays = working(tok_count)
    ins = refs[:-2]
    groups = len(ins) // 2
    for index in range(groups):

        def put(source):
            key_ref[index] = source[0].astype(key_ref.dtype)
            value_ref[index] = source[1].astype(value_ref.dtype)

        pl.when(stays)(functools.partial(put, ins[2 * index]))
        pl.when(jnp.logical_not(stays))(functools.partial(put, ins[2 * index + 1]))
    key_ref[groups] = jnp.zeros_like(key_ref[groups])
    value_ref[groups] = jnp.zeros_like(value_ref[groups])


def call(kernel, outs, *args, scratch=(), limit=16, **kwargs):
    return pl.pallas_call(
        kernel,
        out_shape=outs,
        **kwargs,
        scratch_shapes=scratch,
        cost_estimate=pl.CostEstimate(flops=1, bytes_accessed=1, transcendentals=0),
        compiler_params=pltpu.CompilerParams(vmem_limit_bytes=limit * 1024 * 1024),
    )(*args)


def shape(*dims, dtype=F32):
    return jax.ShapeDtypeStruct(dims, dtype)


def tie(array, after):
    return lax.optimization_barrier((array, after))[0]


def working(tok_count):
    return lax.axis_index("tok") // (tok_count // 2) == lax.axis_index("head") % 2


def bit_of(order):
    bits = [(lax.axis_index(axis) // mask) % 2 for axis, mask in order]
    return jnp.where(lax.axis_index("head") % 2 == 0, bits[0], bits[1]) == 1


def on_device(queries, keys, values, out_grad, fast_init, updates):
    tok_count = lax.axis_size("tok")
    head_count = lax.axis_size("head")
    vid_count = lax.axis_size("vid")
    _, groups, count, _, dim = queries.shape
    half = dim // 2
    rows = 3 * dim
    scale = float(count * tok_count) ** (-0.5)
    share = 2.0 / tok_count
    tok_dims = [("tok", 1 << i) for i in range((tok_count // 2).bit_length() - 1)]
    vid_dims = [("vid", 1 << i) for i in range(vid_count.bit_length() - 1)]
    assert len(tok_dims) >= 1 and 2 << len(tok_dims) == tok_count
    assert 1 << len(vid_dims) == vid_count and head_count % 2 == 0
    assert queries.shape[0] == 1 and queries.shape[3] == 1

    def stays_at(tok, head):
        return tok // (tok_count // 2) == head % 2

    def permute(array, goes):
        pairs = []
        for tok in range(tok_count):
            for head in range(head_count):
                for vid in range(vid_count):
                    there = goes(tok, head, vid)
                    if there is not None:
                        number = lambda t, h, v: (t * head_count + h) * vid_count + v
                        pairs.append((number(tok, head, vid), number(*there)))
        return lax.ppermute(array, ("tok", "head", "vid"), pairs)

    def meet(array, order):
        def goes(tok, head, vid):
            axis, mask = order[head % 2]
            return (tok ^ mask, head, vid) if axis == "tok" else (tok, head, vid ^ mask)

        return permute(array, goes)

    def sibling(array, from_staying=None):
        def goes(tok, head, vid):
            if from_staying is None or stays_at(tok, head) == from_staying:
                return (tok, head ^ 1, vid)

        return permute(array, goes)

    def spread(array):
        def goes(tok, head, vid):
            if stays_at(tok, head):
                return (tok, head ^ 1, vid)
            return (tok ^ (tok_count // 2), head, vid)

        return permute(array, goes)

    def swap(array):
        def goes(tok, head, vid):
            if not stays_at(tok, head):
                return (tok ^ (tok_count // 2), head ^ 1, vid)

        return permute(array, goes)

    def lend(array):
        def goes(tok, head, vid):
            if stays_at(tok, head):
                return (tok ^ (tok_count // 2), head, vid)

        return permute(array, goes)

    flat = lambda array: array.reshape(groups, count, dim)
    q_all, k_all, v_all, c_all = (flat(a) for a in (queries, keys, values, out_grad))
    top = groups - 1
    init = fast_init.reshape(3, dim, dim)
    steps = updates.reshape(groups - 1, 3, dim, dim)

    def send(arrays, index, limit=16):
        return call(
            functools.partial(send_kernel, index, len(arrays)),
            [shape(2, count, dim)] * (len(arrays) // 2),
            *arrays,
            limit=limit,
            in_specs=[pl.BlockSpec(memory_space=pltpu.HBM)] * len(arrays),
            scratch=[
                pltpu.VMEM((len(arrays), count, dim), BF16),
                pltpu.SemaphoreType.DMA((len(arrays),)),
            ],
        )

    own = {top: send([q_all, c_all], top, 60)}
    first = {top: [spread(own[top][0])]}
    init = tie(init, own[top][0])

    low_rows = top * rows + top * VEC
    low_rows += -low_rows % 8
    full, *halves = call(
        prep_kernel,
        [shape(top, 3, dim, dim)] + [shape(rows, half), shape(low_rows, half)] * 2,
        init,
        steps,
        in_specs=[pl.BlockSpec(memory_space=pltpu.HBM)] * 2,
        scratch=[
            pltpu.VMEM(init.shape, BF16),
            pltpu.VMEM(steps.shape, BF16),
            pltpu.SemaphoreType.DMA((groups,)),
        ],
    )

    def chosen(outs, mine, sent):
        return call(functools.partial(weights_kernel, tok_count), outs, mine, sibling(sent))

    (top_weights,) = chosen([shape(rows, half)], halves[0], halves[2])
    (query_grad,) = call(query_kernel, [shape(groups, count, dim, dtype=BF16)], q_all, c_all, init, full)

    def tokens(index, after):
        arrays = []
        for mine, arrived in zip(own[index], first[index]):
            arrays += [mine, arrived, sibling(tie(arrived, after), True)]
        return arrays

    def scratch(index):
        return [pltpu.VMEM((2 * len(own[index]), 2 * count, dim), BF16)]

    both = 2 * count
    (payload,) = call(
        functools.partial(last_kernel, tok_count),
        [shape(rows + PAD, half)],
        *tokens(top, query_grad),
        top_weights,
        scratch=scratch(top),
    )
    weights = chosen(
        [shape(rows, half)] * top + [shape(VEC, half)] * top, halves[1], tie(halves[3], first[top][0])
    )
    factors = list(weights[top:])
    weights = [*weights[:top], top_weights]
    token_grads = {}
    for index in reversed(range(top)):
        own[index] = send([q_all, c_all, k_all, v_all], index)
        first[index] = [spread(tie(array, first[index + 1])) for array in own[index]]
        for at in range(len(tok_dims)):
            arrived = meet(payload, (tok_dims[at], tok_dims[at - 1]))
            if at + 1 < len(tok_dims):
                if at == 0 and index + 1 in token_grads:
                    arrived = tie(arrived, token_grads[index + 1])
                (payload,) = call(add_kernel, [shape(rows + PAD, half)], payload, arrived)
        grad, coef, keyed = call(
            functools.partial(pre_kernel, tok_count),
            [shape(rows, half), shape(7, both, half), shape(2, both, dim, dtype=BF16)],
            *tokens(index, payload),
            weights[index],
            scratch=scratch(index),
        )
        total, sums = call(add_kernel, [shape(rows + PAD, half), shape(PAD, half)], payload, arrived)
        if index > 0:
            out_shapes, order = [shape(rows + PAD, half)], None
        else:
            dims = tok_dims[:1] + vid_dims + tok_dims[1:]
            rs_orders = [dims, dims[-1:] + dims[:-1]]
            order = [rs_orders[0][0], rs_orders[1][0]]
            out_shapes = [shape(3, half, half)] * 2
        *outs, upper, mid = call(
            functools.partial(key_kernel, scale, share, order),
            out_shapes + [shape(rows, half), shape(3, both, half)],
            total,
            sums,
            sibling(sums),
            keyed,
            weights[index + 1],
            weights[index],
            factors[index],
            grad,
            coef,
        )
        payload = outs[0]
        keep, give = call(
            functools.partial(token_kernel, tok_count),
            [shape(2, count, dim)] * 2,
            mid,
            coef,
            weights[index],
            upper,
        )
        (d_tokens,) = call(add_kernel, [shape(2, count, dim)], keep, sibling(give))
        token_grads[index] = d_tokens

    kept, sends = outs
    returned = {index: swap(token_grads[index]) for index in range(top)}

    def wait(array, point):
        for index in range(top):
            if point == (4,0)[min(index, 1)]:
                array = tie(array, returned[index])
        return array

    for at in range(len(dims)):
        arrived = meet(sends, [order[at] for order in rs_orders])
        arrived = wait(arrived, at)
        if at + 1 < len(dims):
            out_shapes = [shape(3, kept.shape[1] // 2, half)] * 2
            order = [order[at + 1] for order in rs_orders]
            kept, sends = call(functools.partial(halve_kernel, order), out_shapes, kept, arrived)
        else:
            (kept,) = call(functools.partial(halve_kernel, None), [shape(*kept.shape)], kept, arrived)
    (pair,) = call(pair_kernel, [shape(2, *kept.shape)], kept, sibling(wait(kept, 2)))
    (block,) = call(
        functools.partial(choose_kernel, tok_count), [shape(*pair.shape)], pair, lend(pair)
    )
    block = wait(block[None], 3)
    ag_orders = [order[::-1] for order in rs_orders]
    for at in range(len(dims)):
        arrived = wait(meet(block, [order[at] for order in ag_orders]), 4 + at)
        if at + 1 < len(dims):
            (pair,) = call(pair_kernel, [shape(2, *block.shape)], block, arrived)
            block = pair.reshape(2 * block.shape[0], *block.shape[1:])
    (init_grad,) = call(
        functools.partial(init_out_kernel, tok_count, rs_orders, ag_orders),
        [shape(3, dim, dim)],
        block,
        arrived,
    )
    arrays = []
    for index in range(top):
        arrays += [token_grads[index], returned[index]]
    key_grad, value_grad = call(
        functools.partial(tokens_out_kernel, tok_count),
        [shape(groups, count, dim, dtype=BF16)] * 2,
        *arrays,
    )
    back = lambda array: array.reshape(queries.shape)
    return back(query_grad), back(key_grad), back(value_grad), init_grad.reshape(fast_init.shape)


def solution(mesh):
    tokens = P("vid", None, "tok", "head", None)
    return jax.shard_map(
        on_device,
        mesh=mesh,
        in_specs=(
            tokens,
            tokens,
            tokens,
            tokens,
            P("head", None, None, None),
            P("vid", None, "head", None, None, None),
        ),
        out_specs=(tokens, tokens, tokens, P("head", None, None, None)),
        check_vma=False,
    )
```

```python
import functools

import jax
import jax.numpy as jnp
from jax import lax
from jax.experimental import pallas as pl
from jax.experimental.pallas import tpu as pltpu
from jax.sharding import PartitionSpec as P

EPS = 1e-06
F32 = jnp.float32
BF16 = jnp.bfloat16
NN = (((1,), (0,)), ((), ()))
NT = (((1,), (1,)), ((), ()))
TN = (((0,), (0,)), ((), ()))
PAD = 8
VEC = 12


def dot(left, right, dims):
    return lax.dot_general(left, right, dims, preferred_element_type=F32)


def split(array):
    high = array.astype(BF16)
    return high, (array - high.astype(F32)).astype(BF16)


def exact_left(left, right, dims):
    return dot(left, right[0], dims) + dot(left, right[1], dims)


def exact_right(left, right, dims):
    return dot(left[0], right, dims) + dot(left[1], right, dims)


def both_split(left, right, dims):
    return (
        dot(left[0], right[0], dims)
        + (dot(left[0], right[1], dims) + dot(left[1], right[0], dims))
    )


def silu_parts(gate):
    sigma = jax.nn.sigmoid(gate)
    rest = 1.0 - sigma
    silu = gate * sigma
    first = sigma * (1.0 + gate * rest)
    second = sigma * rest * (2.0 + gate * (1.0 - 2.0 * sigma))
    return silu, first, second


def rows_of_half(gate, up, down, which):
    dim = gate.shape[0]
    half = dim // 2
    cut = slice(which * half, (which + 1) * half)
    return [
        (0, gate[:, cut]),
        (dim, up[:, cut]),
        (2 * dim, down[cut, :half]),
        (2 * dim + half, down[cut, half:]),
    ]


def load_half(rows, dim):
    half = dim // 2
    gate_up = jnp.concatenate([rows[:dim], rows[dim : 2 * dim]], axis=1)
    down = jnp.concatenate([rows[2 * dim : 2 * dim + half], rows[2 * dim + half :]], axis=1)
    return gate_up, down


def prep_kernel(init_hbm, upd_hbm, full_ref, *refs):
    *halves, init_ref, upd_ref, sems = refs
    levels = range(upd_ref.shape[0])
    pairs = [(init_hbm, init_ref)] + [(upd_hbm.at[at], upd_ref.at[at]) for at in levels]
    fetch(pairs, sems)
    groups = upd_ref.shape[0] + 1
    dim = init_ref.shape[-1]
    half = dim // 2
    core = lax.axis_index("head") % 2
    weights = [init_ref[index].astype(F32) for index in range(3)]
    vectors = []
    levels = []
    for level in range(groups):
        levels.append(weights)
        if level + 1 == groups:
            break
        raised, ratio, cross, inverse = [], [], [], []
        for index in range(3):
            up = weights[index] + upd_ref[level, index].astype(F32)
            old2 = jnp.sum(weights[index] * weights[index], axis=0, keepdims=True) + EPS
            new2 = jnp.sum(up * up, axis=0, keepdims=True) + EPS
            old, new = jnp.sqrt(old2), jnp.sqrt(new2)
            ratio.append(old / new)
            cross.append(1.0 / (old * new))
            inverse.append(1.0 / old2)
            raised.append(up * ratio[index])
        vectors.append((ratio, cross, inverse))
        weights = raised
        for index in range(3):
            full_ref[level, index] = weights[index]

    def write(top_ref, ref, which):
        cut = slice(which * half, (which + 1) * half)
        for level in range(groups):
            target, base = (ref, level * 3 * dim) if level + 1 < groups else (top_ref, 0)
            for row, value in rows_of_half(*levels[level], which):
                target[base + row : base + row + value.shape[0], :] = value
        base = (groups - 1) * 3 * dim
        for kinds in vectors:
            for gate, up, down in kinds:
                for value in (gate[:, cut], up[:, cut], down[:, :half], down[:, half:]):
                    ref[base : base + 1, :] = value
                    base += 1

    @pl.when(core == 0)
    def _():
        write(*halves[:2], 0)
        write(*halves[2:], 1)

    @pl.when(core != 0)
    def _():
        write(*halves[:2], 1)
        write(*halves[2:], 0)


def query_kernel(q_ref, c_ref, init_ref, full_ref, out_ref):
    groups = q_ref.shape[0]
    for index in range(groups):
        query, cot = q_ref[index], c_ref[index]
        if index == 0:
            pieces = [(init_ref[part], None) for part in range(3)]
        else:
            pieces = [split(full_ref[index - 1, part]) for part in range(3)]

        def apply(left, right, dims):
            return dot(left, right[0], dims) if right[1] is None else exact_left(left, right, dims)

        gate = apply(query, pieces[0], NN)
        up = apply(query, pieces[1], NN)
        back = apply(cot, pieces[2], NT)
        silu, first, _ = silu_parts(gate)
        total = None
        for value, piece in ((back * up * first, pieces[0]), (back * silu, pieces[1])):
            value = split(value)
            term = exact_right(value, piece[0], NT) if piece[1] is None else both_split(value, piece, NT)
            total = term if total is None else total + term
        out_ref[index] = total.astype(out_ref.dtype)


def apply_terms(query, cot, rows, dim):
    half = dim // 2
    gate_up, down = load_half(rows, dim)
    raw = exact_left(query, split(gate_up), NN)
    back = exact_left(cot, split(down), NT)
    gate, up = raw[:, :half], raw[:, half:]
    silu, first, _ = silu_parts(gate)
    grads = jnp.concatenate([back * up * first, back * silu], axis=1)
    d_gate_up = exact_left(query, split(grads), TN)
    d_down = exact_right(split(silu * up), cot, TN)
    return d_gate_up, d_down


def fetch(pairs, sems):
    copies = [
        pltpu.make_async_copy(source, target, sems.at[at])
        for at, (source, target) in enumerate(pairs)
    ]
    for copy in copies:
        copy.start()
    for copy in copies:
        copy.wait()


def send_kernel(group, count, *refs):
    ins, outs, (scratch, sems) = refs[:count], refs[count:-2], refs[-2:]
    fetch([(ref.at[group], scratch.at[at]) for at, ref in enumerate(ins)], sems)
    for index in range(count):
        value = scratch[index].astype(F32)
        outs[index // 2][index % 2] = value
        if 2 * len(outs) > count:
            outs[-1][index] = value


def part_kernel(in_ref, *out_refs):
    for at, ref in enumerate(out_refs):
        ref[...] = in_ref[2 * at : 2 * at + 2]


def weights_kernel(tok_count, *refs):
    mine_ref, recv_ref = refs[:2]
    outs = refs[2:]
    stays = working(tok_count)

    def put(source):
        base = 0
        for ref in outs:
            ref[...] = source[base : base + ref.shape[0], :]
            base += ref.shape[0]

    pl.when(stays)(functools.partial(put, mine_ref))
    pl.when(jnp.logical_not(stays))(functools.partial(put, recv_ref))


def pick_tokens(tok_count, token_refs, scratch):
    count = token_refs[0].shape[1]
    stays = working(tok_count)

    def put(base, first, second):
        for index in range(2):
            scratch[base + index, :count, :] = first[index].astype(BF16)
            scratch[base + index, count:, :] = second[index].astype(BF16)

    for base in range(0, scratch.shape[0], 2):
        own_ref, first_ref, late_ref = token_refs[3 * base // 2 :][:3]
        pl.when(stays)(functools.partial(put, base, own_ref, first_ref))
        pl.when(jnp.logical_not(stays))(functools.partial(put, base, first_ref, late_ref))


def last_kernel(tok_count, *refs):
    token_refs, w_ref, out_ref, scratch = refs[:3], *refs[3:]
    dim = scratch.shape[-1]
    half = dim // 2
    pick_tokens(tok_count, token_refs, scratch)
    d_gate_up, d_down = apply_terms(scratch[0], scratch[1], w_ref[...], dim)
    out_ref[:dim, :] = d_gate_up[:, :half]
    out_ref[dim : 2 * dim, :] = d_gate_up[:, half:]
    out_ref[3 * dim :, :] = jnp.zeros((PAD, half), F32)
    for block in range(2):
        value = d_down[:, block * half : (block + 1) * half]
        row = 2 * dim + block * half
        out_ref[row : row + half, :] = value
        out_ref[3 * dim + block : 3 * dim + block + 1, :] = jnp.sum(
            value * w_ref[row : row + half, :], axis=0, keepdims=True
        )


def pre_kernel(tok_count, *refs):
    token_refs, w_ref, grad_ref, coef_ref, tok_ref, scratch = refs[:6], *refs[6:]
    dim = scratch.shape[-1]
    half = dim // 2
    pick_tokens(tok_count, token_refs, scratch)
    query, cot, key, value = (scratch[index] for index in range(4))
    tok_ref[0] = key
    tok_ref[1] = value
    rows = w_ref[...]
    d_gate_up, d_down = apply_terms(query, cot, rows, dim)
    grad_ref[:dim, :] = d_gate_up[:, :half]
    grad_ref[dim : 2 * dim, :] = d_gate_up[:, half:]
    grad_ref[2 * dim : 2 * dim + half, :] = d_down[:, :half]
    grad_ref[2 * dim + half :, :] = d_down[:, half:]
    gate_up, down = load_half(rows, dim)
    raw = exact_left(key, split(gate_up), NN)
    back = exact_left(value, split(down), NT)
    gate, up = raw[:, :half], raw[:, half:]
    silu, first, second = silu_parts(gate)
    coef_ref[0] = first * up
    coef_ref[1] = silu
    coef_ref[2] = back * second * up
    coef_ref[3] = back * first
    coef_ref[4] = back * first * up
    coef_ref[5] = back * silu
    coef_ref[6] = silu * up


def add_kernel(mine_ref, recv_ref, out_ref, *tail_refs):
    total = mine_ref[...] + recv_ref[...]
    out_ref[...] = total
    for ref in tail_refs:
        ref[...] = total[total.shape[0] - ref.shape[0] :]


def carry_kernel(mine_ref, recv_ref, *refs):
    refs[-1][:2] = mine_ref[...] + recv_ref[...]
    if len(refs) == 2:
        refs[1][2:] = refs[0][...]


def key_kernel(scale, share, order, *refs):
    total_ref, sums_ref, sib_ref, tok_ref, new_ref, old_ref, vec_ref, grad_ref, coef_ref = refs[:9]
    *outs, up_ref, mid_ref = refs[9:]
    dim = tok_ref.shape[-1]
    half = dim // 2
    down_sums = sums_ref[...] + sib_ref[...]
    pieces = ((0, dim, 0), (dim, dim, 1), (2 * dim, half, 2), (2 * dim + half, half, 3))
    upper, carried = [], []
    for row, rows, slot in pieces:
        adj = total_ref[row : row + rows, :]
        new = new_ref[row : row + rows, :]
        if slot < 2:
            sums = jnp.sum(new * adj, axis=0, keepdims=True)
        else:
            sums = down_sums[slot - 2 : slot - 1]
        ratio = vec_ref[slot : slot + 1, :]
        cross = vec_ref[4 + slot : 5 + slot, :]
        inverse = vec_ref[8 + slot : 9 + slot, :]
        up_adj = adj * ratio - new * (sums * cross)
        direct = old_ref[row : row + rows, :] * (sums * inverse)
        upper.append(up_adj * scale)
        carried.append((up_adj + direct) * share + grad_ref[row : row + rows, :])
        up_ref[row : row + rows, :] = upper[-1]
    key, value = tok_ref[0], tok_ref[1]
    raw = exact_left(key, split(jnp.concatenate(upper[:2], axis=1)), NN)
    back = exact_left(value, split(jnp.concatenate(upper[2:], axis=1)), NT)
    gate, up = raw[:, :half], raw[:, half:]
    hidden = coef_ref[0] * gate + coef_ref[1] * up
    d_gate = coef_ref[2] * gate + coef_ref[3] * up + coef_ref[0] * back
    d_up = coef_ref[3] * gate + coef_ref[1] * back
    d_gate_up = exact_left(key, split(jnp.concatenate([d_gate, d_up], axis=1)), TN)
    d_down = exact_right(split(hidden), value, TN)
    mid_ref[0] = d_gate
    mid_ref[1] = d_up
    mid_ref[2] = hidden
    results = [
        d_gate_up[:, :half] + carried[0],
        d_gate_up[:, half:] + carried[1],
        d_down[:, :half] + carried[2],
        d_down[:, half:] + carried[3],
    ]
    if order is None:
        (out_ref,) = outs
        out_ref[3 * dim :, :] = jnp.zeros((PAD, half), F32)
        for (row, rows, slot), value in zip(pieces, results):
            out_ref[row : row + rows, :] = value
            if slot >= 2:
                out_ref[3 * dim + slot - 2 : 3 * dim + slot - 1, :] = jnp.sum(
                    value * old_ref[row : row + rows, :], axis=0, keepdims=True
                )
    else:
        halves = [[results[0][:half], results[1][:half], results[2]]]
        halves.append([results[0][half:], results[1][half:], results[3]])
        store_halves(halves, order, *outs)


def store_halves(halves, order, keep_ref, send_ref):
    bit = bit_of(order)

    def put(kept, sent):
        for index in range(3):
            keep_ref[index] = kept[index]
            send_ref[index] = sent[index]

    pl.when(bit)(functools.partial(put, halves[1], halves[0]))
    pl.when(jnp.logical_not(bit))(functools.partial(put, halves[0], halves[1]))


def halve_kernel(order, mine_ref, recv_ref, *outs):
    total = mine_ref[...] + recv_ref[...]
    if order is None:
        outs[0][...] = total
        return
    size = total.shape[1] // 2
    halves = [[total[m, at * size : (at + 1) * size] for m in range(3)] for at in range(2)]
    store_halves(halves, order, *outs)


def pair_kernel(mine_ref, other_ref, out_ref):
    out_ref[0] = mine_ref[...]
    out_ref[1] = other_ref[...]


def choose_kernel(tok_count, own_ref, moved_ref, out_ref):
    stays = working(tok_count)

    def put(source):
        out_ref[...] = source[...]

    pl.when(stays)(functools.partial(put, own_ref))
    pl.when(jnp.logical_not(stays))(functools.partial(put, moved_ref))


def init_out_kernel(tok_count, rs_orders, ag_orders, mine_ref, recv_ref, out_ref):
    dim = out_ref.shape[-1]
    half = dim // 2
    blocks = mine_ref.shape[0]
    size = mine_ref.shape[3]
    steps = len(ag_orders[0])
    stays = working(tok_count)
    for core in range(2):

        @pl.when(lax.axis_index("head") % 2 == core)
        def _():
            for flipped in range(2 * blocks):
                source = mine_ref if flipped < blocks else recv_ref
                where = flipped % blocks
                for slot in range(2):
                    which = core if slot == 0 else 1 - core
                    offset, first = 0, None
                    for at, (axis, mask) in enumerate(rs_orders[which]):
                        bit = (lax.axis_index(axis) // mask) % 2
                        step = ag_orders[core].index((axis, mask))
                        if (flipped >> step) & 1:
                            bit = 1 - bit
                        if at == 0:
                            first = bit
                        else:
                            offset = offset + bit * (dim >> (at + 1))
                    offset = pl.multiple_of(offset, size)
                    low = first * half + offset
                    for index in range(2):
                        out_ref[index, pl.ds(pl.multiple_of(low, size), size), which * half : (which + 1) * half] = (
                            source[where, slot, index]
                        )
                    rows = pl.ds(pl.multiple_of(which * half + offset, size), size)
                    pl.when(first == 0)(functools.partial(put_block, out_ref, rows, slice(0, half), source, where, slot))
                    pl.when(first == 1)(functools.partial(put_block, out_ref, rows, slice(half, dim), source, where, slot))


def put_block(out_ref, rows, lanes, source, where, slot):
    out_ref[2, rows, lanes] = source[where, slot, 2]


def token_kernel(tok_count, mid_ref, coef_ref, w_ref, up_ref, keep_ref, give_ref):
    dim = keep_ref.shape[-1]
    count = keep_ref.shape[1]
    w_gate_up, w_down = load_half(w_ref[...], dim)
    u_gate_up, u_down = load_half(up_ref[...], dim)
    left = jnp.concatenate([mid_ref[0], mid_ref[1]], axis=1)
    d_key = both_split(split(left), split(w_gate_up), NT)
    left = jnp.concatenate([coef_ref[4], coef_ref[5]], axis=1)
    d_key = d_key + both_split(split(left), split(u_gate_up), NT)
    left = jnp.concatenate([mid_ref[2], coef_ref[6]], axis=1)
    right = jnp.concatenate([w_down, u_down], axis=0)
    d_value = both_split(split(left), split(right), NN)

    def put(first, second):
        for index, value in enumerate((d_key, d_value)):
            first[index] = value[:count]
            second[index] = value[count:]

    stays = working(tok_count)
    pl.when(stays)(functools.partial(put, keep_ref, give_ref))
    pl.when(jnp.logical_not(stays))(functools.partial(put, give_ref, keep_ref))


def tokens_out_kernel(tok_count, own_ref, moved_ref, key_ref, value_ref):
    stays = working(tok_count)
    groups = own_ref.shape[0] // 2

    def put(source):
        for index in range(groups):
            key_ref[index] = source[2 * index].astype(key_ref.dtype)
            value_ref[index] = source[2 * index + 1].astype(value_ref.dtype)

    pl.when(stays)(functools.partial(put, own_ref))
    pl.when(jnp.logical_not(stays))(functools.partial(put, moved_ref))
    key_ref[groups] = jnp.zeros_like(key_ref[groups])
    value_ref[groups] = jnp.zeros_like(value_ref[groups])


def call(kernel, outs, *args, scratch=(), limit=16, **kwargs):
    return pl.pallas_call(
        kernel,
        out_shape=outs,
        **kwargs,
        scratch_shapes=scratch,
        cost_estimate=pl.CostEstimate(flops=1, bytes_accessed=1, transcendentals=0),
        compiler_params=pltpu.CompilerParams(vmem_limit_bytes=limit * 1024 * 1024),
    )(*args)


def shape(*dims, dtype=F32):
    return jax.ShapeDtypeStruct(dims, dtype)


def tie(array, after):
    return lax.optimization_barrier((array, after))[0]


def working(tok_count):
    return lax.axis_index("tok") // (tok_count // 2) == lax.axis_index("head") % 2


def bit_of(order):
    bits = [(lax.axis_index(axis) // mask) % 2 for axis, mask in order]
    return jnp.where(lax.axis_index("head") % 2 == 0, bits[0], bits[1]) == 1


def on_device(queries, keys, values, out_grad, fast_init, updates):
    tok_count = lax.axis_size("tok")
    head_count = lax.axis_size("head")
    vid_count = lax.axis_size("vid")
    _, groups, count, _, dim = queries.shape
    half = dim // 2
    rows = 3 * dim
    scale = float(count * tok_count) ** (-0.5)
    share = 2.0 / tok_count
    tok_dims = [("tok", 1 << i) for i in range((tok_count // 2).bit_length() - 1)]
    vid_dims = [("vid", 1 << i) for i in range(vid_count.bit_length() - 1)]
    assert len(tok_dims) >= 1 and 2 << len(tok_dims) == tok_count
    assert 1 << len(vid_dims) == vid_count and head_count % 2 == 0
    assert queries.shape[0] == 1 and queries.shape[3] == 1

    def stays_at(tok, head):
        return tok // (tok_count // 2) == head % 2

    def permute(array, goes):
        pairs = []
        for tok in range(tok_count):
            for head in range(head_count):
                for vid in range(vid_count):
                    there = goes(tok, head, vid)
                    if there is not None:
                        number = lambda t, h, v: (t * head_count + h) * vid_count + v
                        pairs.append((number(tok, head, vid), number(*there)))
        return lax.ppermute(array, ("tok", "head", "vid"), pairs)

    def meet(array, order):
        def goes(tok, head, vid):
            axis, mask = order[head % 2]
            return (tok ^ mask, head, vid) if axis == "tok" else (tok, head, vid ^ mask)

        return permute(array, goes)

    def sibling(array, from_staying=None):
        def goes(tok, head, vid):
            if from_staying is None or stays_at(tok, head) == from_staying:
                return (tok, head ^ 1, vid)

        return permute(array, goes)

    def spread(array):
        def goes(tok, head, vid):
            if stays_at(tok, head):
                return (tok, head ^ 1, vid)
            return (tok ^ (tok_count // 2), head, vid)

        return permute(array, goes)

    def swap(array):
        def goes(tok, head, vid):
            if not stays_at(tok, head):
                return (tok ^ (tok_count // 2), head ^ 1, vid)

        return permute(array, goes)

    def lend(array):
        def goes(tok, head, vid):
            if stays_at(tok, head):
                return (tok ^ (tok_count // 2), head, vid)

        return permute(array, goes)

    flat = lambda array: array.reshape(groups, count, dim)
    q_all, k_all, v_all, c_all = (flat(a) for a in (queries, keys, values, out_grad))
    top = groups - 1
    init = fast_init.reshape(3, dim, dim)
    steps = updates.reshape(groups - 1, 3, dim, dim)

    def send(arrays, index, limit=16, whole=False):
        outs = [shape(2, count, dim)] * (len(arrays) // 2)
        return call(
            functools.partial(send_kernel, index, len(arrays)),
            outs + [shape(len(arrays), count, dim)] * whole,
            *arrays,
            limit=limit,
            in_specs=[pl.BlockSpec(memory_space=pltpu.HBM)] * len(arrays),
            scratch=[
                pltpu.VMEM((len(arrays), count, dim), BF16),
                pltpu.SemaphoreType.DMA((len(arrays),)),
            ],
        )

    own = {top: send([q_all, c_all], top, 60)}
    first = {top: [spread(own[top][0])]}
    init = tie(init, own[top][0])

    low_rows = top * rows + top * VEC
    low_rows += -low_rows % 8
    full, *halves = call(
        prep_kernel,
        [shape(top, 3, dim, dim)] + [shape(rows, half), shape(low_rows, half)] * 2,
        init,
        steps,
        in_specs=[pl.BlockSpec(memory_space=pltpu.HBM)] * 2,
        scratch=[
            pltpu.VMEM(init.shape, BF16),
            pltpu.VMEM(steps.shape, BF16),
            pltpu.SemaphoreType.DMA((groups,)),
        ],
    )

    def chosen(outs, mine, sent):
        return call(functools.partial(weights_kernel, tok_count), outs, mine, sibling(sent))

    (top_weights,) = chosen([shape(rows, half)], halves[0], halves[2])
    (query_grad,) = call(query_kernel, [shape(groups, count, dim, dtype=BF16)], q_all, c_all, init, full)

    def tokens(index, after):
        arrays = []
        if not isinstance(first[index], list):
            pairs = [shape(2, count, dim)] * len(own[index])
            first[index] = call(part_kernel, pairs, first[index])
        for mine, arrived in zip(own[index], first[index]):
            arrays += [mine, arrived, sibling(tie(arrived, after), True)]
        return arrays

    def scratch(index):
        return [pltpu.VMEM((2 * len(own[index]), 2 * count, dim), BF16)]

    both = 2 * count
    (payload,) = call(
        functools.partial(last_kernel, tok_count),
        [shape(rows + PAD, half)],
        *tokens(top, query_grad),
        top_weights,
        scratch=scratch(top),
    )
    weights = chosen(
        [shape(rows, half)] * top + [shape(VEC, half)] * top, halves[1], tie(halves[3], first[top][0])
    )
    factors = list(weights[top:])
    weights = [*weights[:top], top_weights]
    token_grads = []
    for index in reversed(range(top)):
        one = index == 0
        own[index] = send([q_all, c_all, k_all, v_all], index, whole=one)
        if one:
            *own[index], whole = own[index]
            first[index] = spread(tie(whole, first[index + 1]))
        else:
            first[index] = [spread(tie(array, first[index + 1])) for array in own[index]]
        for at in range(len(tok_dims)):
            arrived = meet(payload, (tok_dims[at], tok_dims[at - 1]))
            if at + 1 < len(tok_dims):
                if at == 0 and token_grads:
                    arrived = tie(arrived, (token_grads[-1], first[index]))
                (payload,) = call(add_kernel, [shape(rows + PAD, half)], payload, arrived)
        grad, coef, keyed = call(
            functools.partial(pre_kernel, tok_count),
            [shape(rows, half), shape(7, both, half), shape(2, both, dim, dtype=BF16)],
            *tokens(index, payload),
            weights[index],
            scratch=scratch(index),
        )
        total, sums = call(add_kernel, [shape(rows + PAD, half), shape(PAD, half)], payload, arrived)
        if index > 0:
            out_shapes, order = [shape(rows + PAD, half)], None
        else:
            dims = tok_dims + vid_dims
            rs_orders = [dims, dims[-1:] + dims[:-1]]
            order = [rs_orders[0][0], rs_orders[1][0]]
            out_shapes = [shape(3, half, half)] * 2
        *outs, upper, mid = call(
            functools.partial(key_kernel, scale, share, order),
            out_shapes + [shape(rows, half), shape(3, both, half)],
            total,
            sums,
            sibling(sums),
            keyed,
            weights[index + 1],
            weights[index],
            factors[index],
            grad,
            coef,
        )
        payload = outs[0]
        keep, give = call(
            functools.partial(token_kernel, tok_count),
            [shape(2, count, dim)] * 2,
            mid,
            coef,
            weights[index],
            upper,
        )
        done = 2 * (top - index)
        (d_tokens,) = call(
            carry_kernel, [shape(done, count, dim)], keep, sibling(give), *token_grads[-1:]
        )
        token_grads.append(d_tokens)

    kept, sends = outs
    returned = swap(token_grads[-1])

    def wait(array, point):
        return tie(array, returned) if point == 5 else array

    for at in range(len(dims)):
        arrived = meet(sends, [order[at] for order in rs_orders])
        arrived = wait(arrived, at)
        if at + 1 < len(dims):
            out_shapes = [shape(3, kept.shape[1] // 2, half)] * 2
            order = [order[at + 1] for order in rs_orders]
            kept, sends = call(functools.partial(halve_kernel, order), out_shapes, kept, arrived)
        else:
            (kept,) = call(functools.partial(halve_kernel, None), [shape(*kept.shape)], kept, arrived)
    (pair,) = call(pair_kernel, [shape(2, *kept.shape)], kept, sibling(wait(kept, 2)))
    (block,) = call(
        functools.partial(choose_kernel, tok_count), [shape(*pair.shape)], pair, lend(pair)
    )
    block = wait(block[None], 3)
    ag_orders = [order[::-1] for order in rs_orders]
    for at in range(len(dims)):
        arrived = wait(meet(block, [order[at] for order in ag_orders]), 4 + at)
        if at + 1 < len(dims):
            (pair,) = call(pair_kernel, [shape(2, *block.shape)], block, arrived)
            block = pair.reshape(2 * block.shape[0], *block.shape[1:])
    (init_grad,) = call(
        functools.partial(init_out_kernel, tok_count, rs_orders, ag_orders),
        [shape(3, dim, dim)],
        block,
        arrived,
    )
    key_grad, value_grad = call(
        functools.partial(tokens_out_kernel, tok_count),
        [shape(groups, count, dim, dtype=BF16)] * 2,
        token_grads[-1],
        returned,
    )
    back = lambda array: array.reshape(queries.shape)
    return back(query_grad), back(key_grad), back(value_grad), init_grad.reshape(fast_init.shape)


def solution(mesh):
    tokens = P("vid", None, "tok", "head", None)
    return jax.shard_map(
        on_device,
        mesh=mesh,
        in_specs=(
            tokens,
            tokens,
            tokens,
            tokens,
            P("head", None, None, None),
            P("vid", None, "head", None, None, None),
        ),
        out_specs=(tokens, tokens, tokens, P("head", None, None, None)),
        check_vma=False,
    )
```

```python
import functools

import jax
import jax.numpy as jnp
from jax import lax
from jax.experimental import pallas as pl
from jax.experimental.pallas import tpu as pltpu
from jax.sharding import PartitionSpec as P

EPS = 1e-06
F32 = jnp.float32
BF16 = jnp.bfloat16
NN = (((1,), (0,)), ((), ()))
NT = (((1,), (1,)), ((), ()))
TN = (((0,), (0,)), ((), ()))
PAD = 8
VEC = 12


def dot(left, right, dims):
    return lax.dot_general(left, right, dims, preferred_element_type=F32)


def split(array):
    high = array.astype(BF16)
    return high, (array - high.astype(F32)).astype(BF16)


def exact_left(left, right, dims):
    return dot(left, right[0], dims) + dot(left, right[1], dims)


def exact_right(left, right, dims):
    return dot(left[0], right, dims) + dot(left[1], right, dims)


def both_split(left, right, dims):
    return (
        dot(left[0], right[0], dims)
        + (dot(left[0], right[1], dims) + dot(left[1], right[0], dims))
    )


def silu_parts(gate):
    sigma = jax.nn.sigmoid(gate)
    rest = 1.0 - sigma
    silu = gate * sigma
    first = sigma * (1.0 + gate * rest)
    second = sigma * rest * (2.0 + gate * (1.0 - 2.0 * sigma))
    return silu, first, second


def rows_of_half(gate, up, down, which):
    dim = gate.shape[0]
    half = dim // 2
    cut = slice(which * half, (which + 1) * half)
    return [
        (0, gate[:, cut]),
        (dim, up[:, cut]),
        (2 * dim, down[cut, :half]),
        (2 * dim + half, down[cut, half:]),
    ]


def load_half(rows, dim):
    half = dim // 2
    gate_up = jnp.concatenate([rows[:dim], rows[dim : 2 * dim]], axis=1)
    down = jnp.concatenate([rows[2 * dim : 2 * dim + half], rows[2 * dim + half :]], axis=1)
    return gate_up, down


def prep_kernel(init_hbm, upd_hbm, full_ref, *refs):
    *halves, init_ref, upd_ref, sems = refs
    levels = range(upd_ref.shape[0])
    pairs = [(init_hbm, init_ref)] + [(upd_hbm.at[at], upd_ref.at[at]) for at in levels]
    fetch(pairs, sems)
    groups = upd_ref.shape[0] + 1
    dim = init_ref.shape[-1]
    half = dim // 2
    core = lax.axis_index("head") % 2
    weights = [init_ref[index].astype(F32) for index in range(3)]
    vectors = []
    levels = []
    for level in range(groups):
        levels.append(weights)
        if level + 1 == groups:
            break
        raised, ratio, cross, inverse = [], [], [], []
        for index in range(3):
            up = weights[index] + upd_ref[level, index].astype(F32)
            old2 = jnp.sum(weights[index] * weights[index], axis=0, keepdims=True) + EPS
            new2 = jnp.sum(up * up, axis=0, keepdims=True) + EPS
            old, new = jnp.sqrt(old2), jnp.sqrt(new2)
            ratio.append(old / new)
            cross.append(1.0 / (old * new))
            inverse.append(1.0 / old2)
            raised.append(up * ratio[index])
        vectors.append((ratio, cross, inverse))
        weights = raised
        for index in range(3):
            full_ref[level, index] = weights[index]

    def write(top_ref, ref, which):
        cut = slice(which * half, (which + 1) * half)
        for level in range(groups):
            target, base = (ref, level * 3 * dim) if level + 1 < groups else (top_ref, 0)
            for row, value in rows_of_half(*levels[level], which):
                target[base + row : base + row + value.shape[0], :] = value
        base = (groups - 1) * 3 * dim
        for kinds in vectors:
            for gate, up, down in kinds:
                for value in (gate[:, cut], up[:, cut], down[:, :half], down[:, half:]):
                    ref[base : base + 1, :] = value
                    base += 1

    @pl.when(core == 0)
    def _():
        write(*halves[:2], 0)
        write(*halves[2:], 1)

    @pl.when(core != 0)
    def _():
        write(*halves[:2], 1)
        write(*halves[2:], 0)


def query_kernel(q_ref, c_ref, init_ref, full_ref, out_ref):
    groups = q_ref.shape[0]
    for index in range(groups):
        query, cot = q_ref[index], c_ref[index]
        if index == 0:
            pieces = [(init_ref[part], None) for part in range(3)]
        else:
            pieces = [split(full_ref[index - 1, part]) for part in range(3)]

        def apply(left, right, dims):
            return dot(left, right[0], dims) if right[1] is None else exact_left(left, right, dims)

        gate = apply(query, pieces[0], NN)
        up = apply(query, pieces[1], NN)
        back = apply(cot, pieces[2], NT)
        silu, first, _ = silu_parts(gate)
        total = None
        for value, piece in ((back * up * first, pieces[0]), (back * silu, pieces[1])):
            value = split(value)
            term = exact_right(value, piece[0], NT) if piece[1] is None else both_split(value, piece, NT)
            total = term if total is None else total + term
        out_ref[index] = total.astype(out_ref.dtype)


def apply_terms(query, cot, rows, dim):
    half = dim // 2
    gate_up, down = load_half(rows, dim)
    raw = exact_left(query, split(gate_up), NN)
    back = exact_left(cot, split(down), NT)
    gate, up = raw[:, :half], raw[:, half:]
    silu, first, _ = silu_parts(gate)
    grads = jnp.concatenate([back * up * first, back * silu], axis=1)
    d_gate_up = exact_left(query, split(grads), TN)
    d_down = exact_right(split(silu * up), cot, TN)
    return d_gate_up, d_down


def fetch(pairs, sems):
    copies = [
        pltpu.make_async_copy(source, target, sems.at[at])
        for at, (source, target) in enumerate(pairs)
    ]
    for copy in copies:
        copy.start()
    for copy in copies:
        copy.wait()


def send_kernel(group, count, *refs):
    ins, outs, (scratch, sems) = refs[:count], refs[count:-2], refs[-2:]
    fetch([(ref.at[group], scratch.at[at]) for at, ref in enumerate(ins)], sems)
    for index in range(count):
        value = scratch[index].astype(F32)
        outs[index // 2][index % 2] = value
        if 2 * len(outs) > count:
            outs[-1][index] = value


def part_kernel(in_ref, *out_refs):
    for at, ref in enumerate(out_refs):
        ref[...] = in_ref[2 * at : 2 * at + 2]


def weights_kernel(tok_count, *refs):
    mine_ref, recv_ref = refs[:2]
    outs = refs[2:]
    stays = working(tok_count)

    def put(source):
        base = 0
        for ref in outs:
            ref[...] = source[base : base + ref.shape[0], :]
            base += ref.shape[0]

    pl.when(stays)(functools.partial(put, mine_ref))
    pl.when(jnp.logical_not(stays))(functools.partial(put, recv_ref))


def pick_tokens(tok_count, token_refs, scratch):
    count = token_refs[0].shape[1]
    stays = working(tok_count)

    def put(base, first, second):
        for index in range(2):
            scratch[base + index, :count, :] = first[index].astype(BF16)
            scratch[base + index, count:, :] = second[index].astype(BF16)

    for base in range(0, scratch.shape[0], 2):
        own_ref, first_ref, late_ref = token_refs[3 * base // 2 :][:3]
        pl.when(stays)(functools.partial(put, base, own_ref, first_ref))
        pl.when(jnp.logical_not(stays))(functools.partial(put, base, first_ref, late_ref))


def last_kernel(tok_count, *refs):
    token_refs, w_ref, out_ref, scratch = refs[:3], *refs[3:]
    dim = scratch.shape[-1]
    half = dim // 2
    pick_tokens(tok_count, token_refs, scratch)
    d_gate_up, d_down = apply_terms(scratch[0], scratch[1], w_ref[...], dim)
    out_ref[:dim, :] = d_gate_up[:, :half]
    out_ref[dim : 2 * dim, :] = d_gate_up[:, half:]
    out_ref[3 * dim :, :] = jnp.zeros((PAD, half), F32)
    for block in range(2):
        value = d_down[:, block * half : (block + 1) * half]
        row = 2 * dim + block * half
        out_ref[row : row + half, :] = value
        out_ref[3 * dim + block : 3 * dim + block + 1, :] = jnp.sum(
            value * w_ref[row : row + half, :], axis=0, keepdims=True
        )


def pre_kernel(tok_count, *refs):
    token_refs, w_ref, grad_ref, coef_ref, tok_ref, scratch = refs[:6], *refs[6:]
    dim = scratch.shape[-1]
    half = dim // 2
    pick_tokens(tok_count, token_refs, scratch)
    query, cot, key, value = (scratch[index] for index in range(4))
    tok_ref[0] = key
    tok_ref[1] = value
    rows = w_ref[...]
    d_gate_up, d_down = apply_terms(query, cot, rows, dim)
    grad_ref[:dim, :] = d_gate_up[:, :half]
    grad_ref[dim : 2 * dim, :] = d_gate_up[:, half:]
    grad_ref[2 * dim : 2 * dim + half, :] = d_down[:, :half]
    grad_ref[2 * dim + half :, :] = d_down[:, half:]
    gate_up, down = load_half(rows, dim)
    raw = exact_left(key, split(gate_up), NN)
    back = exact_left(value, split(down), NT)
    gate, up = raw[:, :half], raw[:, half:]
    silu, first, second = silu_parts(gate)
    coef_ref[0] = first * up
    coef_ref[1] = silu
    coef_ref[2] = back * second * up
    coef_ref[3] = back * first
    coef_ref[4] = back * first * up
    coef_ref[5] = back * silu
    coef_ref[6] = silu * up


def add_kernel(mine_ref, recv_ref, out_ref, *tail_refs):
    total = mine_ref[...] + recv_ref[...]
    out_ref[...] = total
    for ref in tail_refs:
        ref[...] = total[total.shape[0] - ref.shape[0] :]


def carry_kernel(mine_ref, recv_ref, *refs):
    refs[-1][:2] = mine_ref[...] + recv_ref[...]
    if len(refs) == 2:
        refs[1][2:] = refs[0][...]


def key_kernel(scale, share, order, *refs):
    total_ref, sums_ref, sib_ref, tok_ref, new_ref, old_ref, vec_ref, grad_ref, coef_ref = refs[:9]
    *outs, up_ref, mid_ref = refs[9:]
    dim = tok_ref.shape[-1]
    half = dim // 2
    down_sums = sums_ref[...] + sib_ref[...]
    pieces = ((0, dim, 0), (dim, dim, 1), (2 * dim, half, 2), (2 * dim + half, half, 3))
    upper, carried = [], []
    for row, rows, slot in pieces:
        adj = total_ref[row : row + rows, :]
        new = new_ref[row : row + rows, :]
        if slot < 2:
            sums = jnp.sum(new * adj, axis=0, keepdims=True)
        else:
            sums = down_sums[slot - 2 : slot - 1]
        ratio = vec_ref[slot : slot + 1, :]
        cross = vec_ref[4 + slot : 5 + slot, :]
        inverse = vec_ref[8 + slot : 9 + slot, :]
        up_adj = adj * ratio - new * (sums * cross)
        direct = old_ref[row : row + rows, :] * (sums * inverse)
        upper.append(up_adj * scale)
        carried.append((up_adj + direct) * share + grad_ref[row : row + rows, :])
        up_ref[row : row + rows, :] = upper[-1]
    key, value = tok_ref[0], tok_ref[1]
    raw = exact_left(key, split(jnp.concatenate(upper[:2], axis=1)), NN)
    back = exact_left(value, split(jnp.concatenate(upper[2:], axis=1)), NT)
    gate, up = raw[:, :half], raw[:, half:]
    hidden = coef_ref[0] * gate + coef_ref[1] * up
    d_gate = coef_ref[2] * gate + coef_ref[3] * up + coef_ref[0] * back
    d_up = coef_ref[3] * gate + coef_ref[1] * back
    d_gate_up = exact_left(key, split(jnp.concatenate([d_gate, d_up], axis=1)), TN)
    d_down = exact_right(split(hidden), value, TN)
    mid_ref[0] = d_gate
    mid_ref[1] = d_up
    mid_ref[2] = hidden
    results = [
        d_gate_up[:, :half] + carried[0],
        d_gate_up[:, half:] + carried[1],
        d_down[:, :half] + carried[2],
        d_down[:, half:] + carried[3],
    ]
    if order is None:
        (out_ref,) = outs
        out_ref[3 * dim :, :] = jnp.zeros((PAD, half), F32)
        for (row, rows, slot), value in zip(pieces, results):
            out_ref[row : row + rows, :] = value
            if slot >= 2:
                out_ref[3 * dim + slot - 2 : 3 * dim + slot - 1, :] = jnp.sum(
                    value * old_ref[row : row + rows, :], axis=0, keepdims=True
                )
    else:
        halves = [[results[0][:half], results[1][:half], results[2]]]
        halves.append([results[0][half:], results[1][half:], results[3]])
        store_halves(halves, order, *outs)


def store_halves(halves, order, keep_ref, send_ref):
    bit = bit_of(order)

    def put(kept, sent):
        for index in range(3):
            keep_ref[index] = kept[index]
            send_ref[index] = sent[index]

    pl.when(bit)(functools.partial(put, halves[1], halves[0]))
    pl.when(jnp.logical_not(bit))(functools.partial(put, halves[0], halves[1]))


def halve_kernel(order, mine_ref, recv_ref, *outs):
    total = mine_ref[...] + recv_ref[...]
    if order is None:
        outs[0][...] = total
        return
    size = total.shape[1] // 2
    halves = [[total[m, at * size : (at + 1) * size] for m in range(3)] for at in range(2)]
    store_halves(halves, order, *outs)


def pair_kernel(mine_ref, other_ref, out_ref):
    out_ref[0] = mine_ref[...]
    out_ref[1] = other_ref[...]


def choose_kernel(tok_count, own_ref, moved_ref, out_ref):
    stays = working(tok_count)

    def put(source):
        out_ref[...] = source[...]

    pl.when(stays)(functools.partial(put, own_ref))
    pl.when(jnp.logical_not(stays))(functools.partial(put, moved_ref))


def init_out_kernel(tok_count, rs_orders, ag_orders, mine_ref, recv_ref, out_ref):
    dim = out_ref.shape[-1]
    half = dim // 2
    blocks = mine_ref.shape[0]
    size = mine_ref.shape[3]
    steps = len(ag_orders[0])
    stays = working(tok_count)
    for core in range(2):

        @pl.when(lax.axis_index("head") % 2 == core)
        def _():
            for flipped in range(2 * blocks):
                source = mine_ref if flipped < blocks else recv_ref
                where = flipped % blocks
                for slot in range(2):
                    which = core if slot == 0 else 1 - core
                    offset, first = 0, None
                    for at, (axis, mask) in enumerate(rs_orders[which]):
                        bit = (lax.axis_index(axis) // mask) % 2
                        step = ag_orders[core].index((axis, mask))
                        if (flipped >> step) & 1:
                            bit = 1 - bit
                        if at == 0:
                            first = bit
                        else:
                            offset = offset + bit * (dim >> (at + 1))
                    offset = pl.multiple_of(offset, size)
                    low = first * half + offset
                    for index in range(2):
                        out_ref[index, pl.ds(pl.multiple_of(low, size), size), which * half : (which + 1) * half] = (
                            source[where, slot, index]
                        )
                    rows = pl.ds(pl.multiple_of(which * half + offset, size), size)
                    pl.when(first == 0)(functools.partial(put_block, out_ref, rows, slice(0, half), source, where, slot))
                    pl.when(first == 1)(functools.partial(put_block, out_ref, rows, slice(half, dim), source, where, slot))


def put_block(out_ref, rows, lanes, source, where, slot):
    out_ref[2, rows, lanes] = source[where, slot, 2]


def token_kernel(tok_count, mid_ref, coef_ref, w_ref, up_ref, keep_ref, give_ref):
    dim = keep_ref.shape[-1]
    count = keep_ref.shape[1]
    w_gate_up, w_down = load_half(w_ref[...], dim)
    u_gate_up, u_down = load_half(up_ref[...], dim)
    left = jnp.concatenate([mid_ref[0], mid_ref[1]], axis=1)
    d_key = both_split(split(left), split(w_gate_up), NT)
    left = jnp.concatenate([coef_ref[4], coef_ref[5]], axis=1)
    d_key = d_key + both_split(split(left), split(u_gate_up), NT)
    left = jnp.concatenate([mid_ref[2], coef_ref[6]], axis=1)
    right = jnp.concatenate([w_down, u_down], axis=0)
    d_value = both_split(split(left), split(right), NN)

    def put(first, second):
        for index, value in enumerate((d_key, d_value)):
            first[index] = value[:count]
            second[index] = value[count:]

    stays = working(tok_count)
    pl.when(stays)(functools.partial(put, keep_ref, give_ref))
    pl.when(jnp.logical_not(stays))(functools.partial(put, give_ref, keep_ref))


def tokens_out_kernel(tok_count, own_ref, moved_ref, key_ref, value_ref):
    stays = working(tok_count)
    groups = own_ref.shape[0] // 2

    def put(source):
        for index in range(groups):
            key_ref[index] = source[2 * index].astype(key_ref.dtype)
            value_ref[index] = source[2 * index + 1].astype(value_ref.dtype)

    pl.when(stays)(functools.partial(put, own_ref))
    pl.when(jnp.logical_not(stays))(functools.partial(put, moved_ref))
    key_ref[groups] = jnp.zeros_like(key_ref[groups])
    value_ref[groups] = jnp.zeros_like(value_ref[groups])


def call(kernel, outs, *args, scratch=(), limit=16, flops=1, **kwargs):
    return pl.pallas_call(
        kernel,
        out_shape=outs,
        **kwargs,
        scratch_shapes=scratch,
        cost_estimate=pl.CostEstimate(flops=flops, bytes_accessed=1, transcendentals=0),
        compiler_params=pltpu.CompilerParams(vmem_limit_bytes=limit * 1024 * 1024),
    )(*args)


def shape(*dims, dtype=F32):
    return jax.ShapeDtypeStruct(dims, dtype)


def tie(array, after):
    return lax.optimization_barrier((array, after))[0]


def working(tok_count):
    return lax.axis_index("tok") // (tok_count // 2) == lax.axis_index("head") % 2


def bit_of(order):
    bits = [(lax.axis_index(axis) // mask) % 2 for axis, mask in order]
    return jnp.where(lax.axis_index("head") % 2 == 0, bits[0], bits[1]) == 1


def on_device(queries, keys, values, out_grad, fast_init, updates):
    tok_count = lax.axis_size("tok")
    head_count = lax.axis_size("head")
    vid_count = lax.axis_size("vid")
    _, groups, count, _, dim = queries.shape
    half = dim // 2
    rows = 3 * dim
    scale = float(count * tok_count) ** (-0.5)
    share = 2.0 / tok_count
    tok_dims = [("tok", 1 << i) for i in range((tok_count // 2).bit_length() - 1)]
    vid_dims = [("vid", 1 << i) for i in range(vid_count.bit_length() - 1)]
    assert len(tok_dims) >= 1 and 2 << len(tok_dims) == tok_count
    assert 1 << len(vid_dims) == vid_count and head_count % 2 == 0
    assert queries.shape[0] == 1 and queries.shape[3] == 1

    def stays_at(tok, head):
        return tok // (tok_count // 2) == head % 2

    def permute(array, goes):
        pairs = []
        for tok in range(tok_count):
            for head in range(head_count):
                for vid in range(vid_count):
                    there = goes(tok, head, vid)
                    if there is not None:
                        number = lambda t, h, v: (t * head_count + h) * vid_count + v
                        pairs.append((number(tok, head, vid), number(*there)))
        return lax.ppermute(array, ("tok", "head", "vid"), pairs)

    def meet(array, order):
        def goes(tok, head, vid):
            axis, mask = order[head % 2]
            return (tok ^ mask, head, vid) if axis == "tok" else (tok, head, vid ^ mask)

        return permute(array, goes)

    def sibling(array, from_staying=None):
        def goes(tok, head, vid):
            if from_staying is None or stays_at(tok, head) == from_staying:
                return (tok, head ^ 1, vid)

        return permute(array, goes)

    def spread(array):
        def goes(tok, head, vid):
            if stays_at(tok, head):
                return (tok, head ^ 1, vid)
            return (tok ^ (tok_count // 2), head, vid)

        return permute(array, goes)

    def swap(array):
        def goes(tok, head, vid):
            if not stays_at(tok, head):
                return (tok ^ (tok_count // 2), head ^ 1, vid)

        return permute(array, goes)

    def lend(array):
        def goes(tok, head, vid):
            if stays_at(tok, head):
                return (tok ^ (tok_count // 2), head, vid)

        return permute(array, goes)

    flat = lambda array: array.reshape(groups, count, dim)
    q_all, k_all, v_all, c_all = (flat(a) for a in (queries, keys, values, out_grad))
    top = groups - 1
    init = fast_init.reshape(3, dim, dim)
    steps = updates.reshape(groups - 1, 3, dim, dim)

    def send(arrays, index, limit=16, whole=False):
        outs = [shape(2, count, dim)] * (len(arrays) // 2)
        return call(
            functools.partial(send_kernel, index, len(arrays)),
            outs + [shape(len(arrays), count, dim)] * whole,
            *arrays,
            limit=limit,
            in_specs=[pl.BlockSpec(memory_space=pltpu.HBM)] * len(arrays),
            scratch=[
                pltpu.VMEM((len(arrays), count, dim), BF16),
                pltpu.SemaphoreType.DMA((len(arrays),)),
            ],
        )

    own = {top: send([q_all, c_all], top, 60)}
    first = {top: [spread(own[top][0])]}
    init = tie(init, own[top][0])

    low_rows = top * rows + top * VEC
    low_rows += -low_rows % 8
    full, *halves = call(
        prep_kernel,
        [shape(top, 3, dim, dim)] + [shape(rows, half), shape(low_rows, half)] * 2,
        init,
        steps,
        in_specs=[pl.BlockSpec(memory_space=pltpu.HBM)] * 2,
        scratch=[
            pltpu.VMEM(init.shape, BF16),
            pltpu.VMEM(steps.shape, BF16),
            pltpu.SemaphoreType.DMA((groups,)),
        ],
    )

    def chosen(outs, mine, sent):
        return call(functools.partial(weights_kernel, tok_count), outs, mine, sibling(sent))

    (top_weights,) = chosen([shape(rows, half)], halves[0], halves[2])
    (query_grad,) = call(query_kernel, [shape(groups, count, dim, dtype=BF16)], q_all, c_all, init, full)

    def tokens(index, after):
        arrays = []
        if not isinstance(first[index], list):
            pairs = [shape(2, count, dim)] * len(own[index])
            first[index] = call(part_kernel, pairs, first[index], flops=4000000000)
        for mine, arrived in zip(own[index], first[index]):
            arrays += [mine, arrived, sibling(tie(arrived, after), True)]
        return arrays

    def scratch(index):
        return [pltpu.VMEM((2 * len(own[index]), 2 * count, dim), BF16)]

    both = 2 * count
    (payload,) = call(
        functools.partial(last_kernel, tok_count),
        [shape(rows + PAD, half)],
        *tokens(top, query_grad),
        top_weights,
        scratch=scratch(top),
    )
    weights = chosen(
        [shape(rows, half)] * top + [shape(VEC, half)] * top, halves[1], tie(halves[3], first[top][0])
    )
    factors = list(weights[top:])
    weights = [*weights[:top], top_weights]
    token_grads = []
    for index in reversed(range(top)):
        one = True
        own[index] = send([q_all, c_all, k_all, v_all], index, whole=one)
        if one:
            *own[index], whole = own[index]
            first[index] = spread(tie(whole, first[index + 1]))
        else:
            first[index] = [spread(tie(array, first[index + 1])) for array in own[index]]
        for at in range(len(tok_dims)):
            arrived = meet(payload, (tok_dims[at], tok_dims[at - 1]))
            if at + 1 < len(tok_dims):
                if at == 0 and token_grads:
                    arrived = tie(arrived, token_grads[-1])
                (payload,) = call(add_kernel, [shape(rows + PAD, half)], payload, arrived)
        grad, coef, keyed = call(
            functools.partial(pre_kernel, tok_count),
            [shape(rows, half), shape(7, both, half), shape(2, both, dim, dtype=BF16)],
            *tokens(index, payload),
            weights[index],
            scratch=scratch(index),
        )
        total, sums = call(add_kernel, [shape(rows + PAD, half), shape(PAD, half)], payload, arrived)
        if index > 0:
            out_shapes, order = [shape(rows + PAD, half)], None
        else:
            dims = tok_dims + vid_dims
            rs_orders = [dims, dims[-1:] + dims[:-1]]
            order = [rs_orders[0][0], rs_orders[1][0]]
            out_shapes = [shape(3, half, half)] * 2
        *outs, upper, mid = call(
            functools.partial(key_kernel, scale, share, order),
            out_shapes + [shape(rows, half), shape(3, both, half)],
            total,
            sums,
            sibling(sums),
            keyed,
            weights[index + 1],
            weights[index],
            factors[index],
            grad,
            coef,
        )
        payload = outs[0]
        keep, give = call(
            functools.partial(token_kernel, tok_count),
            [shape(2, count, dim)] * 2,
            mid,
            coef,
            weights[index],
            upper,
        )
        done = 2 * (top - index)
        (d_tokens,) = call(
            carry_kernel, [shape(done, count, dim)], keep, sibling(give), *token_grads[-1:]
        )
        token_grads.append(d_tokens)

    kept, sends = outs
    returned = swap(token_grads[-1])

    def wait(array, point):
        return tie(array, returned) if point == 5 else array

    for at in range(len(dims)):
        arrived = meet(sends, [order[at] for order in rs_orders])
        arrived = wait(arrived, at)
        if at + 1 < len(dims):
            out_shapes = [shape(3, kept.shape[1] // 2, half)] * 2
            order = [order[at + 1] for order in rs_orders]
            kept, sends = call(functools.partial(halve_kernel, order), out_shapes, kept, arrived)
        else:
            (kept,) = call(functools.partial(halve_kernel, None), [shape(*kept.shape)], kept, arrived)
    (pair,) = call(pair_kernel, [shape(2, *kept.shape)], kept, sibling(wait(kept, 2)))
    (block,) = call(
        functools.partial(choose_kernel, tok_count), [shape(*pair.shape)], pair, lend(pair)
    )
    block = wait(block[None], 3)
    ag_orders = [order[::-1] for order in rs_orders]
    for at in range(len(dims)):
        arrived = wait(meet(block, [order[at] for order in ag_orders]), 4 + at)
        if at + 1 < len(dims):
            (pair,) = call(pair_kernel, [shape(2, *block.shape)], block, arrived)
            block = pair.reshape(2 * block.shape[0], *block.shape[1:])
    (init_grad,) = call(
        functools.partial(init_out_kernel, tok_count, rs_orders, ag_orders),
        [shape(3, dim, dim)],
        block,
        arrived,
    )
    key_grad, value_grad = call(
        functools.partial(tokens_out_kernel, tok_count),
        [shape(groups, count, dim, dtype=BF16)] * 2,
        token_grads[-1],
        returned,
    )
    back = lambda array: array.reshape(queries.shape)
    return back(query_grad), back(key_grad), back(value_grad), init_grad.reshape(fast_init.shape)


def solution(mesh):
    tokens = P("vid", None, "tok", "head", None)
    return jax.shard_map(
        on_device,
        mesh=mesh,
        in_specs=(
            tokens,
            tokens,
            tokens,
            tokens,
            P("head", None, None, None),
            P("vid", None, "head", None, None, None),
        ),
        out_specs=(tokens, tokens, tokens, P("head", None, None, None)),
        check_vma=False,
    )
```

```python
import functools

import jax
import jax.numpy as jnp
from jax import lax
from jax.experimental import pallas as pl
from jax.experimental.pallas import tpu as pltpu
from jax.sharding import PartitionSpec as P

EPS = 1e-06
F32 = jnp.float32
BF16 = jnp.bfloat16
NN = (((1,), (0,)), ((), ()))
NT = (((1,), (1,)), ((), ()))
TN = (((0,), (0,)), ((), ()))
PAD = 8
VEC = 12


def dot(left, right, dims):
    return lax.dot_general(left, right, dims, preferred_element_type=F32)


def split(array):
    high = array.astype(BF16)
    return high, (array - high.astype(F32)).astype(BF16)


def exact_left(left, right, dims):
    return dot(left, right[0], dims) + dot(left, right[1], dims)


def exact_right(left, right, dims):
    return dot(left[0], right, dims) + dot(left[1], right, dims)


def both_split(left, right, dims):
    return (
        dot(left[0], right[0], dims)
        + (dot(left[0], right[1], dims) + dot(left[1], right[0], dims))
    )


def silu_parts(gate):
    sigma = jax.nn.sigmoid(gate)
    rest = 1.0 - sigma
    silu = gate * sigma
    first = sigma * (1.0 + gate * rest)
    second = sigma * rest * (2.0 + gate * (1.0 - 2.0 * sigma))
    return silu, first, second


def rows_of_half(gate, up, down, which):
    dim = gate.shape[0]
    half = dim // 2
    cut = slice(which * half, (which + 1) * half)
    return [
        (0, gate[:, cut]),
        (dim, up[:, cut]),
        (2 * dim, down[cut, :half]),
        (2 * dim + half, down[cut, half:]),
    ]


def load_half(rows, dim):
    half = dim // 2
    gate_up = jnp.concatenate([rows[:dim], rows[dim : 2 * dim]], axis=1)
    down = jnp.concatenate([rows[2 * dim : 2 * dim + half], rows[2 * dim + half :]], axis=1)
    return gate_up, down


def prep_kernel(init_hbm, upd_hbm, full_ref, *refs):
    *halves, init_ref, upd_ref, sems = refs
    levels = range(upd_ref.shape[0])
    pairs = [(init_hbm, init_ref)] + [(upd_hbm.at[at], upd_ref.at[at]) for at in levels]
    fetch(pairs, sems)
    groups = upd_ref.shape[0] + 1
    dim = init_ref.shape[-1]
    half = dim // 2
    core = lax.axis_index("head") % 2
    weights = [init_ref[index].astype(F32) for index in range(3)]
    vectors = []
    levels = []
    for level in range(groups):
        levels.append(weights)
        if level + 1 == groups:
            break
        raised, ratio, cross, inverse = [], [], [], []
        for index in range(3):
            up = weights[index] + upd_ref[level, index].astype(F32)
            old2 = jnp.sum(weights[index] * weights[index], axis=0, keepdims=True) + EPS
            new2 = jnp.sum(up * up, axis=0, keepdims=True) + EPS
            old, new = jnp.sqrt(old2), jnp.sqrt(new2)
            ratio.append(old / new)
            cross.append(1.0 / (old * new))
            inverse.append(1.0 / old2)
            raised.append(up * ratio[index])
        vectors.append((ratio, cross, inverse))
        weights = raised
        for index in range(3):
            full_ref[level, index] = weights[index]

    def write(top_ref, ref, which):
        cut = slice(which * half, (which + 1) * half)
        for level in range(groups):
            target, base = (ref, level * 3 * dim) if level + 1 < groups else (top_ref, 0)
            for row, value in rows_of_half(*levels[level], which):
                target[base + row : base + row + value.shape[0], :] = value
        base = (groups - 1) * 3 * dim
        for kinds in vectors:
            for gate, up, down in kinds:
                for value in (gate[:, cut], up[:, cut], down[:, :half], down[:, half:]):
                    ref[base : base + 1, :] = value
                    base += 1

    @pl.when(core == 0)
    def _():
        write(*halves[:2], 0)
        write(*halves[2:], 1)

    @pl.when(core != 0)
    def _():
        write(*halves[:2], 1)
        write(*halves[2:], 0)


def query_kernel(q_ref, c_ref, init_ref, full_ref, out_ref):
    groups = q_ref.shape[0]
    for index in range(groups):
        query, cot = q_ref[index], c_ref[index]
        if index == 0:
            pieces = [(init_ref[part], None) for part in range(3)]
        else:
            pieces = [split(full_ref[index - 1, part]) for part in range(3)]

        def apply(left, right, dims):
            return dot(left, right[0], dims) if right[1] is None else exact_left(left, right, dims)

        gate = apply(query, pieces[0], NN)
        up = apply(query, pieces[1], NN)
        back = apply(cot, pieces[2], NT)
        silu, first, _ = silu_parts(gate)
        total = None
        for value, piece in ((back * up * first, pieces[0]), (back * silu, pieces[1])):
            value = split(value)
            term = exact_right(value, piece[0], NT) if piece[1] is None else both_split(value, piece, NT)
            total = term if total is None else total + term
        out_ref[index] = total.astype(out_ref.dtype)


def apply_terms(query, cot, rows, dim):
    half = dim // 2
    gate_up, down = load_half(rows, dim)
    raw = exact_left(query, split(gate_up), NN)
    back = exact_left(cot, split(down), NT)
    gate, up = raw[:, :half], raw[:, half:]
    silu, first, _ = silu_parts(gate)
    grads = jnp.concatenate([back * up * first, back * silu], axis=1)
    d_gate_up = exact_left(query, split(grads), TN)
    d_down = exact_right(split(silu * up), cot, TN)
    return d_gate_up, d_down


def fetch(pairs, sems):
    copies = [
        pltpu.make_async_copy(source, target, sems.at[at])
        for at, (source, target) in enumerate(pairs)
    ]
    for copy in copies:
        copy.start()
    for copy in copies:
        copy.wait()


def send_kernel(group, count, *refs):
    ins, outs, (scratch, sems) = refs[:count], refs[count:-2], refs[-2:]
    fetch([(ref.at[group], scratch.at[at]) for at, ref in enumerate(ins)], sems)
    for index in range(count):
        value = scratch[index].astype(F32)
        outs[index // 2][index % 2] = value
        if 2 * len(outs) > count:
            outs[-1][index] = value


def part_kernel(in_ref, *out_refs):
    for at, ref in enumerate(out_refs):
        ref[...] = in_ref[2 * at : 2 * at + 2]


def weights_kernel(tok_count, *refs):
    mine_ref, recv_ref = refs[:2]
    outs = refs[2:]
    stays = working(tok_count)

    def put(source):
        base = 0
        for ref in outs:
            ref[...] = source[base : base + ref.shape[0], :]
            base += ref.shape[0]

    pl.when(stays)(functools.partial(put, mine_ref))
    pl.when(jnp.logical_not(stays))(functools.partial(put, recv_ref))


def pick_tokens(tok_count, token_refs, scratch):
    count = token_refs[0].shape[1]
    stays = working(tok_count)

    def put(base, first, second):
        for index in range(2):
            scratch[base + index, :count, :] = first[index].astype(BF16)
            scratch[base + index, count:, :] = second[index].astype(BF16)

    for base in range(0, scratch.shape[0], 2):
        own_ref, first_ref, late_ref = token_refs[3 * base // 2 :][:3]
        pl.when(stays)(functools.partial(put, base, own_ref, first_ref))
        pl.when(jnp.logical_not(stays))(functools.partial(put, base, first_ref, late_ref))


def last_kernel(tok_count, *refs):
    token_refs, w_ref, out_ref, scratch = refs[:3], *refs[3:]
    dim = scratch.shape[-1]
    half = dim // 2
    pick_tokens(tok_count, token_refs, scratch)
    d_gate_up, d_down = apply_terms(scratch[0], scratch[1], w_ref[...], dim)
    out_ref[:dim, :] = d_gate_up[:, :half]
    out_ref[dim : 2 * dim, :] = d_gate_up[:, half:]
    out_ref[3 * dim :, :] = jnp.zeros((PAD, half), F32)
    for block in range(2):
        value = d_down[:, block * half : (block + 1) * half]
        row = 2 * dim + block * half
        out_ref[row : row + half, :] = value
        out_ref[3 * dim + block : 3 * dim + block + 1, :] = jnp.sum(
            value * w_ref[row : row + half, :], axis=0, keepdims=True
        )


def pre_kernel(tok_count, *refs):
    token_refs, w_ref, grad_ref, coef_ref, tok_ref, scratch = refs[:6], *refs[6:]
    dim = scratch.shape[-1]
    half = dim // 2
    pick_tokens(tok_count, token_refs, scratch)
    query, cot, key, value = (scratch[index] for index in range(4))
    tok_ref[0] = key
    tok_ref[1] = value
    rows = w_ref[...]
    d_gate_up, d_down = apply_terms(query, cot, rows, dim)
    grad_ref[:dim, :] = d_gate_up[:, :half]
    grad_ref[dim : 2 * dim, :] = d_gate_up[:, half:]
    grad_ref[2 * dim : 2 * dim + half, :] = d_down[:, :half]
    grad_ref[2 * dim + half :, :] = d_down[:, half:]
    gate_up, down = load_half(rows, dim)
    raw = exact_left(key, split(gate_up), NN)
    back = exact_left(value, split(down), NT)
    gate, up = raw[:, :half], raw[:, half:]
    silu, first, second = silu_parts(gate)
    coef_ref[0] = first * up
    coef_ref[1] = silu
    coef_ref[2] = back * second * up
    coef_ref[3] = back * first
    coef_ref[4] = back * first * up
    coef_ref[5] = back * silu
    coef_ref[6] = silu * up


def add_kernel(mine_ref, recv_ref, out_ref, *tail_refs):
    total = mine_ref[...] + recv_ref[...]
    out_ref[...] = total
    for ref in tail_refs:
        ref[...] = total[total.shape[0] - ref.shape[0] :]


def carry_kernel(mine_ref, recv_ref, *refs):
    refs[-1][:2] = mine_ref[...] + recv_ref[...]
    if len(refs) == 2:
        refs[1][2:] = refs[0][...]


def key_kernel(scale, share, order, *refs):
    total_ref, sums_ref, sib_ref, tok_ref, new_ref, old_ref, vec_ref, grad_ref, coef_ref = refs[:9]
    *outs, up_ref, mid_ref = refs[9:]
    dim = tok_ref.shape[-1]
    half = dim // 2
    down_sums = sums_ref[...] + sib_ref[...]
    pieces = ((0, dim, 0), (dim, dim, 1), (2 * dim, half, 2), (2 * dim + half, half, 3))
    upper, carried = [], []
    for row, rows, slot in pieces:
        adj = total_ref[row : row + rows, :]
        new = new_ref[row : row + rows, :]
        if slot < 2:
            sums = jnp.sum(new * adj, axis=0, keepdims=True)
        else:
            sums = down_sums[slot - 2 : slot - 1]
        ratio = vec_ref[slot : slot + 1, :]
        cross = vec_ref[4 + slot : 5 + slot, :]
        inverse = vec_ref[8 + slot : 9 + slot, :]
        up_adj = adj * ratio - new * (sums * cross)
        direct = old_ref[row : row + rows, :] * (sums * inverse)
        upper.append(up_adj * scale)
        carried.append((up_adj + direct) * share + grad_ref[row : row + rows, :])
        up_ref[row : row + rows, :] = upper[-1]
    key, value = tok_ref[0], tok_ref[1]
    raw = exact_left(key, split(jnp.concatenate(upper[:2], axis=1)), NN)
    back = exact_left(value, split(jnp.concatenate(upper[2:], axis=1)), NT)
    gate, up = raw[:, :half], raw[:, half:]
    hidden = coef_ref[0] * gate + coef_ref[1] * up
    d_gate = coef_ref[2] * gate + coef_ref[3] * up + coef_ref[0] * back
    d_up = coef_ref[3] * gate + coef_ref[1] * back
    d_gate_up = exact_left(key, split(jnp.concatenate([d_gate, d_up], axis=1)), TN)
    d_down = exact_right(split(hidden), value, TN)
    mid_ref[0] = d_gate
    mid_ref[1] = d_up
    mid_ref[2] = hidden
    results = [
        d_gate_up[:, :half] + carried[0],
        d_gate_up[:, half:] + carried[1],
        d_down[:, :half] + carried[2],
        d_down[:, half:] + carried[3],
    ]
    if order is None:
        (out_ref,) = outs
        out_ref[3 * dim :, :] = jnp.zeros((PAD, half), F32)
        for (row, rows, slot), value in zip(pieces, results):
            out_ref[row : row + rows, :] = value
            if slot >= 2:
                out_ref[3 * dim + slot - 2 : 3 * dim + slot - 1, :] = jnp.sum(
                    value * old_ref[row : row + rows, :], axis=0, keepdims=True
                )
    else:
        halves = [[results[0][:half], results[1][:half], results[2]]]
        halves.append([results[0][half:], results[1][half:], results[3]])
        store_halves(halves, order, *outs)


def store_halves(halves, order, keep_ref, send_ref):
    bit = bit_of(order)

    def put(kept, sent):
        for index in range(3):
            keep_ref[index] = kept[index]
            send_ref[index] = sent[index]

    pl.when(bit)(functools.partial(put, halves[1], halves[0]))
    pl.when(jnp.logical_not(bit))(functools.partial(put, halves[0], halves[1]))


def halve_kernel(order, mine_ref, recv_ref, *outs):
    total = mine_ref[...] + recv_ref[...]
    if order is None:
        outs[0][...] = total
        return
    size = total.shape[1] // 2
    halves = [[total[m, at * size : (at + 1) * size] for m in range(3)] for at in range(2)]
    store_halves(halves, order, *outs)


def pair_kernel(mine_ref, other_ref, out_ref):
    out_ref[0] = mine_ref[...]
    out_ref[1] = other_ref[...]


def choose_kernel(tok_count, own_ref, moved_ref, out_ref):
    stays = working(tok_count)

    def put(source):
        out_ref[...] = source[...]

    pl.when(stays)(functools.partial(put, own_ref))
    pl.when(jnp.logical_not(stays))(functools.partial(put, moved_ref))


def init_out_kernel(tok_count, rs_orders, ag_orders, mine_ref, recv_ref, out_ref):
    dim = out_ref.shape[-1]
    half = dim // 2
    blocks = mine_ref.shape[0]
    size = mine_ref.shape[3]
    steps = len(ag_orders[0])
    stays = working(tok_count)
    for core in range(2):

        @pl.when(lax.axis_index("head") % 2 == core)
        def _():
            for flipped in range(2 * blocks):
                source = mine_ref if flipped < blocks else recv_ref
                where = flipped % blocks
                for slot in range(2):
                    which = core if slot == 0 else 1 - core
                    offset, first = 0, None
                    for at, (axis, mask) in enumerate(rs_orders[which]):
                        bit = (lax.axis_index(axis) // mask) % 2
                        step = ag_orders[core].index((axis, mask))
                        if (flipped >> step) & 1:
                            bit = 1 - bit
                        if at == 0:
                            first = bit
                        else:
                            offset = offset + bit * (dim >> (at + 1))
                    offset = pl.multiple_of(offset, size)
                    low = first * half + offset
                    for index in range(2):
                        out_ref[index, pl.ds(pl.multiple_of(low, size), size), which * half : (which + 1) * half] = (
                            source[where, slot, index]
                        )
                    rows = pl.ds(pl.multiple_of(which * half + offset, size), size)
                    pl.when(first == 0)(functools.partial(put_block, out_ref, rows, slice(0, half), source, where, slot))
                    pl.when(first == 1)(functools.partial(put_block, out_ref, rows, slice(half, dim), source, where, slot))


def put_block(out_ref, rows, lanes, source, where, slot):
    out_ref[2, rows, lanes] = source[where, slot, 2]


def token_kernel(tok_count, mid_ref, coef_ref, w_ref, up_ref, keep_ref, give_ref):
    dim = keep_ref.shape[-1]
    count = keep_ref.shape[1]
    w_gate_up, w_down = load_half(w_ref[...], dim)
    u_gate_up, u_down = load_half(up_ref[...], dim)
    left = jnp.concatenate([mid_ref[0], mid_ref[1]], axis=1)
    d_key = both_split(split(left), split(w_gate_up), NT)
    left = jnp.concatenate([coef_ref[4], coef_ref[5]], axis=1)
    d_key = d_key + both_split(split(left), split(u_gate_up), NT)
    left = jnp.concatenate([mid_ref[2], coef_ref[6]], axis=1)
    right = jnp.concatenate([w_down, u_down], axis=0)
    d_value = both_split(split(left), split(right), NN)

    def put(first, second):
        for index, value in enumerate((d_key, d_value)):
            first[index] = value[:count]
            second[index] = value[count:]

    stays = working(tok_count)
    pl.when(stays)(functools.partial(put, keep_ref, give_ref))
    pl.when(jnp.logical_not(stays))(functools.partial(put, give_ref, keep_ref))


def tokens_out_kernel(tok_count, own_ref, moved_ref, key_ref, value_ref):
    stays = working(tok_count)
    groups = own_ref.shape[0] // 2

    def put(source):
        for index in range(groups):
            key_ref[index] = source[2 * index].astype(key_ref.dtype)
            value_ref[index] = source[2 * index + 1].astype(value_ref.dtype)

    pl.when(stays)(functools.partial(put, own_ref))
    pl.when(jnp.logical_not(stays))(functools.partial(put, moved_ref))
    key_ref[groups] = jnp.zeros_like(key_ref[groups])
    value_ref[groups] = jnp.zeros_like(value_ref[groups])


def call(kernel, outs, *args, scratch=(), limit=16, flops=1, **kwargs):
    return pl.pallas_call(
        kernel,
        out_shape=outs,
        **kwargs,
        scratch_shapes=scratch,
        cost_estimate=pl.CostEstimate(flops=flops, bytes_accessed=1, transcendentals=0),
        compiler_params=pltpu.CompilerParams(vmem_limit_bytes=limit * 1024 * 1024),
    )(*args)


def shape(*dims, dtype=F32):
    return jax.ShapeDtypeStruct(dims, dtype)


def tie(array, after):
    return lax.optimization_barrier((array, after))[0]


def working(tok_count):
    return lax.axis_index("tok") // (tok_count // 2) == lax.axis_index("head") % 2


def bit_of(order):
    bits = [(lax.axis_index(axis) // mask) % 2 for axis, mask in order]
    return jnp.where(lax.axis_index("head") % 2 == 0, bits[0], bits[1]) == 1


def on_device(queries, keys, values, out_grad, fast_init, updates):
    tok_count = lax.axis_size("tok")
    head_count = lax.axis_size("head")
    vid_count = lax.axis_size("vid")
    _, groups, count, _, dim = queries.shape
    half = dim // 2
    rows = 3 * dim
    scale = float(count * tok_count) ** (-0.5)
    share = 2.0 / tok_count
    tok_dims = [("tok", 1 << i) for i in range((tok_count // 2).bit_length() - 1)]
    vid_dims = [("vid", 1 << i) for i in range(vid_count.bit_length() - 1)]
    assert len(tok_dims) >= 1 and 2 << len(tok_dims) == tok_count
    assert 1 << len(vid_dims) == vid_count and head_count % 2 == 0
    assert queries.shape[0] == 1 and queries.shape[3] == 1

    def stays_at(tok, head):
        return tok // (tok_count // 2) == head % 2

    def permute(array, goes):
        pairs = []
        for tok in range(tok_count):
            for head in range(head_count):
                for vid in range(vid_count):
                    there = goes(tok, head, vid)
                    if there is not None:
                        number = lambda t, h, v: (t * head_count + h) * vid_count + v
                        pairs.append((number(tok, head, vid), number(*there)))
        return lax.ppermute(array, ("tok", "head", "vid"), pairs)

    def meet(array, order):
        def goes(tok, head, vid):
            axis, mask = order[head % 2]
            return (tok ^ mask, head, vid) if axis == "tok" else (tok, head, vid ^ mask)

        return permute(array, goes)

    def sibling(array, from_staying=None):
        def goes(tok, head, vid):
            if from_staying is None or stays_at(tok, head) == from_staying:
                return (tok, head ^ 1, vid)

        return permute(array, goes)

    def spread(array):
        def goes(tok, head, vid):
            if stays_at(tok, head):
                return (tok, head ^ 1, vid)
            return (tok ^ (tok_count // 2), head, vid)

        return permute(array, goes)

    def swap(array):
        def goes(tok, head, vid):
            if not stays_at(tok, head):
                return (tok ^ (tok_count // 2), head ^ 1, vid)

        return permute(array, goes)

    def lend(array):
        def goes(tok, head, vid):
            if stays_at(tok, head):
                return (tok ^ (tok_count // 2), head, vid)
            return (tok, head ^ 1, vid)

        return permute(array, goes)

    flat = lambda array: array.reshape(groups, count, dim)
    q_all, k_all, v_all, c_all = (flat(a) for a in (queries, keys, values, out_grad))
    top = groups - 1
    init = fast_init.reshape(3, dim, dim)
    steps = updates.reshape(groups - 1, 3, dim, dim)

    def send(arrays, index, limit=16, whole=False):
        outs = [shape(2, count, dim)] * (len(arrays) // 2)
        return call(
            functools.partial(send_kernel, index, len(arrays)),
            outs + [shape(len(arrays), count, dim)] * whole,
            *arrays,
            limit=limit,
            in_specs=[pl.BlockSpec(memory_space=pltpu.HBM)] * len(arrays),
            scratch=[
                pltpu.VMEM((len(arrays), count, dim), BF16),
                pltpu.SemaphoreType.DMA((len(arrays),)),
            ],
        )

    own = {top: send([q_all, c_all], top, 60)}
    first = {top: [spread(own[top][0])]}
    init = tie(init, own[top][0])

    low_rows = top * rows + top * VEC
    low_rows += -low_rows % 8
    full, *halves = call(
        prep_kernel,
        [shape(top, 3, dim, dim)] + [shape(rows, half), shape(low_rows, half)] * 2,
        init,
        steps,
        in_specs=[pl.BlockSpec(memory_space=pltpu.HBM)] * 2,
        scratch=[
            pltpu.VMEM(init.shape, BF16),
            pltpu.VMEM(steps.shape, BF16),
            pltpu.SemaphoreType.DMA((groups,)),
        ],
    )

    def chosen(outs, mine, sent):
        return call(functools.partial(weights_kernel, tok_count), outs, mine, sibling(sent))

    (top_weights,) = chosen([shape(rows, half)], halves[0], halves[2])
    (query_grad,) = call(query_kernel, [shape(groups, count, dim, dtype=BF16)], q_all, c_all, init, full)

    def tokens(index, after):
        arrays = []
        if not isinstance(first[index], list):
            pairs = [shape(2, count, dim)] * len(own[index])
            first[index] = call(part_kernel, pairs, first[index], flops=4000000000)
        for mine, arrived in zip(own[index], first[index]):
            arrays += [mine, arrived, sibling(tie(arrived, after), True)]
        return arrays

    def scratch(index):
        return [pltpu.VMEM((2 * len(own[index]), 2 * count, dim), BF16)]

    both = 2 * count
    (payload,) = call(
        functools.partial(last_kernel, tok_count),
        [shape(rows + PAD, half)],
        *tokens(top, query_grad),
        top_weights,
        scratch=scratch(top),
    )
    weights = chosen(
        [shape(rows, half)] * top + [shape(VEC, half)] * top, halves[1], tie(halves[3], first[top][0])
    )
    factors = list(weights[top:])
    weights = [*weights[:top], top_weights]
    token_grads = []
    for index in reversed(range(top)):
        one = True
        own[index] = send([q_all, c_all, k_all, v_all], index, whole=one)
        if one:
            *own[index], whole = own[index]
            first[index] = spread(tie(whole, first[index + 1]))
        else:
            first[index] = [spread(tie(array, first[index + 1])) for array in own[index]]
        for at in range(len(tok_dims)):
            arrived = meet(payload, (tok_dims[at], tok_dims[at - 1]))
            if at + 1 < len(tok_dims):
                if at == 0 and token_grads:
                    arrived = tie(arrived, token_grads[-1])
                (payload,) = call(add_kernel, [shape(rows + PAD, half)], payload, arrived)
        grad, coef, keyed = call(
            functools.partial(pre_kernel, tok_count),
            [shape(rows, half), shape(7, both, half), shape(2, both, dim, dtype=BF16)],
            *tokens(index, payload),
            weights[index],
            scratch=scratch(index),
        )
        total, sums = call(add_kernel, [shape(rows + PAD, half), shape(PAD, half)], payload, arrived)
        if index > 0:
            out_shapes, order = [shape(rows + PAD, half)], None
        else:
            dims = tok_dims + vid_dims
            rs_orders = [dims, dims[-1:] + dims[:-1]]
            order = [rs_orders[0][0], rs_orders[1][0]]
            out_shapes = [shape(3, half, half)] * 2
        *outs, upper, mid = call(
            functools.partial(key_kernel, scale, share, order),
            out_shapes + [shape(rows, half), shape(3, both, half)],
            total,
            sums,
            sibling(sums),
            keyed,
            weights[index + 1],
            weights[index],
            factors[index],
            grad,
            coef,
        )
        payload = outs[0]
        keep, give = call(
            functools.partial(token_kernel, tok_count),
            [shape(2, count, dim)] * 2,
            mid,
            coef,
            weights[index],
            upper,
        )
        done = 2 * (top - index)
        (d_tokens,) = call(
            carry_kernel, [shape(done, count, dim)], keep, sibling(give), *token_grads[-1:]
        )
        token_grads.append(d_tokens)

    kept, sends = outs
    returned = swap(token_grads[-1])

    def wait(array, point):
        return tie(array, returned) if point == 5 else array

    for at in range(len(dims)):
        arrived = meet(sends, [order[at] for order in rs_orders])
        arrived = wait(arrived, at)
        if at + 1 < len(dims):
            out_shapes = [shape(3, kept.shape[1] // 2, half)] * 2
            order = [order[at + 1] for order in rs_orders]
            kept, sends = call(functools.partial(halve_kernel, order), out_shapes, kept, arrived)
        else:
            (kept,) = call(functools.partial(halve_kernel, None), [shape(*kept.shape)], kept, arrived)
    (pair,) = call(pair_kernel, [shape(2, *kept.shape)], kept, sibling(wait(kept, 2)))
    (block,) = call(
        functools.partial(choose_kernel, tok_count), [shape(*pair.shape)], pair, lend(pair)
    )
    block = wait(block[None], 3)
    ag_orders = [order[::-1] for order in rs_orders]
    for at in range(len(dims)):
        arrived = wait(meet(block, [order[at] for order in ag_orders]), 4 + at)
        if at + 1 < len(dims):
            (pair,) = call(pair_kernel, [shape(2, *block.shape)], block, arrived)
            block = pair.reshape(2 * block.shape[0], *block.shape[1:])
    (init_grad,) = call(
        functools.partial(init_out_kernel, tok_count, rs_orders, ag_orders),
        [shape(3, dim, dim)],
        block,
        arrived,
    )
    key_grad, value_grad = call(
        functools.partial(tokens_out_kernel, tok_count),
        [shape(groups, count, dim, dtype=BF16)] * 2,
        token_grads[-1],
        returned,
    )
    back = lambda array: array.reshape(queries.shape)
    return back(query_grad), back(key_grad), back(value_grad), init_grad.reshape(fast_init.shape)


def solution(mesh):
    tokens = P("vid", None, "tok", "head", None)
    return jax.shard_map(
        on_device,
        mesh=mesh,
        in_specs=(
            tokens,
            tokens,
            tokens,
            tokens,
            P("head", None, None, None),
            P("vid", None, "head", None, None, None),
        ),
        out_specs=(tokens, tokens, tokens, P("head", None, None, None)),
        check_vma=False,
    )
```

```python
import functools

import jax
import jax.numpy as jnp
from jax import lax
from jax.experimental import pallas as pl
from jax.experimental.pallas import tpu as pltpu
from jax.sharding import PartitionSpec as P

EPS = 1e-06
F32 = jnp.float32
BF16 = jnp.bfloat16
NN = (((1,), (0,)), ((), ()))
NT = (((1,), (1,)), ((), ()))
TN = (((0,), (0,)), ((), ()))
PAD = 8
VEC = 12


def dot(left, right, dims):
    return lax.dot_general(left, right, dims, preferred_element_type=F32)


def split(array):
    high = array.astype(BF16)
    return high, (array - high.astype(F32)).astype(BF16)


def exact_left(left, right, dims):
    return dot(left, right[0], dims) + dot(left, right[1], dims)


def exact_right(left, right, dims):
    return dot(left[0], right, dims) + dot(left[1], right, dims)


def both_split(left, right, dims):
    return (
        dot(left[0], right[0], dims)
        + (dot(left[0], right[1], dims) + dot(left[1], right[0], dims))
    )


def silu_parts(gate):
    sigma = jax.nn.sigmoid(gate)
    rest = 1.0 - sigma
    silu = gate * sigma
    first = sigma * (1.0 + gate * rest)
    second = sigma * rest * (2.0 + gate * (1.0 - 2.0 * sigma))
    return silu, first, second


def rows_of_half(gate, up, down, which):
    dim = gate.shape[0]
    half = dim // 2
    cut = slice(which * half, (which + 1) * half)
    return [
        (0, gate[:, cut]),
        (dim, up[:, cut]),
        (2 * dim, down[cut, :half]),
        (2 * dim + half, down[cut, half:]),
    ]


def load_half(rows, dim):
    half = dim // 2
    gate_up = jnp.concatenate([rows[:dim], rows[dim : 2 * dim]], axis=1)
    down = jnp.concatenate([rows[2 * dim : 2 * dim + half], rows[2 * dim + half :]], axis=1)
    return gate_up, down


def prep_kernel(init_hbm, upd_hbm, full_ref, *refs):
    *halves, init_ref, upd_ref, sems = refs
    levels = range(upd_ref.shape[0])
    pairs = [(init_hbm, init_ref)] + [(upd_hbm.at[at], upd_ref.at[at]) for at in levels]
    fetch(pairs, sems)
    groups = upd_ref.shape[0] + 1
    dim = init_ref.shape[-1]
    half = dim // 2
    core = lax.axis_index("head") % 2
    weights = [init_ref[index].astype(F32) for index in range(3)]
    vectors = []
    levels = []
    for level in range(groups):
        levels.append(weights)
        if level + 1 == groups:
            break
        raised, ratio, cross, inverse = [], [], [], []
        for index in range(3):
            up = weights[index] + upd_ref[level, index].astype(F32)
            old2 = jnp.sum(weights[index] * weights[index], axis=0, keepdims=True) + EPS
            new2 = jnp.sum(up * up, axis=0, keepdims=True) + EPS
            old, new = jnp.sqrt(old2), jnp.sqrt(new2)
            ratio.append(old / new)
            cross.append(1.0 / (old * new))
            inverse.append(1.0 / old2)
            raised.append(up * ratio[index])
        vectors.append((ratio, cross, inverse))
        weights = raised
        for index in range(3):
            full_ref[level, index] = weights[index]

    def write(top_ref, ref, which):
        cut = slice(which * half, (which + 1) * half)
        for level in range(groups):
            target, base = (ref, level * 3 * dim) if level + 1 < groups else (top_ref, 0)
            for row, value in rows_of_half(*levels[level], which):
                target[base + row : base + row + value.shape[0], :] = value
        base = (groups - 1) * 3 * dim
        for kinds in vectors:
            for gate, up, down in kinds:
                for value in (gate[:, cut], up[:, cut], down[:, :half], down[:, half:]):
                    ref[base : base + 1, :] = value
                    base += 1

    @pl.when(core == 0)
    def _():
        write(*halves[:2], 0)
        write(*halves[2:], 1)

    @pl.when(core != 0)
    def _():
        write(*halves[:2], 1)
        write(*halves[2:], 0)


def query_kernel(q_ref, c_ref, init_ref, full_ref, out_ref):
    groups = q_ref.shape[0]
    for index in range(groups):
        query, cot = q_ref[index], c_ref[index]
        if index == 0:
            pieces = [(init_ref[part], None) for part in range(3)]
        else:
            pieces = [split(full_ref[index - 1, part]) for part in range(3)]

        def apply(left, right, dims):
            return dot(left, right[0], dims) if right[1] is None else exact_left(left, right, dims)

        gate = apply(query, pieces[0], NN)
        up = apply(query, pieces[1], NN)
        back = apply(cot, pieces[2], NT)
        silu, first, _ = silu_parts(gate)
        total = None
        for value, piece in ((back * up * first, pieces[0]), (back * silu, pieces[1])):
            value = split(value)
            term = exact_right(value, piece[0], NT) if piece[1] is None else both_split(value, piece, NT)
            total = term if total is None else total + term
        out_ref[index] = total.astype(out_ref.dtype)


def apply_terms(query, cot, rows, dim):
    half = dim // 2
    gate_up, down = load_half(rows, dim)
    raw = exact_left(query, split(gate_up), NN)
    back = exact_left(cot, split(down), NT)
    gate, up = raw[:, :half], raw[:, half:]
    silu, first, _ = silu_parts(gate)
    grads = jnp.concatenate([back * up * first, back * silu], axis=1)
    d_gate_up = exact_left(query, split(grads), TN)
    d_down = exact_right(split(silu * up), cot, TN)
    return d_gate_up, d_down


def fetch(pairs, sems):
    copies = [
        pltpu.make_async_copy(source, target, sems.at[at])
        for at, (source, target) in enumerate(pairs)
    ]
    for copy in copies:
        copy.start()
    for copy in copies:
        copy.wait()


def send_kernel(group, count, *refs):
    ins, outs, (scratch, sems) = refs[:count], refs[count:-2], refs[-2:]
    fetch([(ref.at[group], scratch.at[at]) for at, ref in enumerate(ins)], sems)
    for index in range(count):
        value = scratch[index].astype(F32)
        outs[index // 2][index % 2] = value
        if 2 * len(outs) > count:
            outs[-1][index] = value


def part_kernel(in_ref, *out_refs):
    for at, ref in enumerate(out_refs):
        ref[...] = in_ref[2 * at : 2 * at + 2]


def weights_kernel(tok_count, *refs):
    mine_ref, recv_ref = refs[:2]
    outs = refs[2:]
    stays = working(tok_count)

    def put(source):
        base = 0
        for ref in outs:
            ref[...] = source[base : base + ref.shape[0], :]
            base += ref.shape[0]

    pl.when(stays)(functools.partial(put, mine_ref))
    pl.when(jnp.logical_not(stays))(functools.partial(put, recv_ref))


def pick_tokens(tok_count, token_refs, scratch):
    count = token_refs[0].shape[1]
    stays = working(tok_count)

    def put(base, first, second):
        for index in range(2):
            scratch[base + index, :count, :] = first[index].astype(BF16)
            scratch[base + index, count:, :] = second[index].astype(BF16)

    for base in range(0, scratch.shape[0], 2):
        own_ref, first_ref, late_ref = token_refs[3 * base // 2 :][:3]
        pl.when(stays)(functools.partial(put, base, own_ref, first_ref))
        pl.when(jnp.logical_not(stays))(functools.partial(put, base, first_ref, late_ref))


def last_kernel(tok_count, *refs):
    token_refs, w_ref, out_ref, scratch = refs[:3], *refs[3:]
    dim = scratch.shape[-1]
    half = dim // 2
    pick_tokens(tok_count, token_refs, scratch)
    d_gate_up, d_down = apply_terms(scratch[0], scratch[1], w_ref[...], dim)
    out_ref[:dim, :] = d_gate_up[:, :half]
    out_ref[dim : 2 * dim, :] = d_gate_up[:, half:]
    out_ref[3 * dim :, :] = jnp.zeros((PAD, half), F32)
    for block in range(2):
        value = d_down[:, block * half : (block + 1) * half]
        row = 2 * dim + block * half
        out_ref[row : row + half, :] = value
        out_ref[3 * dim + block : 3 * dim + block + 1, :] = jnp.sum(
            value * w_ref[row : row + half, :], axis=0, keepdims=True
        )


def pre_kernel(tok_count, *refs):
    token_refs, w_ref, grad_ref, coef_ref, tok_ref, scratch = refs[:6], *refs[6:]
    dim = scratch.shape[-1]
    half = dim // 2
    pick_tokens(tok_count, token_refs, scratch)
    query, cot, key, value = (scratch[index] for index in range(4))
    tok_ref[0] = key
    tok_ref[1] = value
    rows = w_ref[...]
    d_gate_up, d_down = apply_terms(query, cot, rows, dim)
    grad_ref[:dim, :] = d_gate_up[:, :half]
    grad_ref[dim : 2 * dim, :] = d_gate_up[:, half:]
    grad_ref[2 * dim : 2 * dim + half, :] = d_down[:, :half]
    grad_ref[2 * dim + half :, :] = d_down[:, half:]
    gate_up, down = load_half(rows, dim)
    raw = exact_left(key, split(gate_up), NN)
    back = exact_left(value, split(down), NT)
    gate, up = raw[:, :half], raw[:, half:]
    silu, first, second = silu_parts(gate)
    coef_ref[0] = first * up
    coef_ref[1] = silu
    coef_ref[2] = back * second * up
    coef_ref[3] = back * first
    coef_ref[4] = back * first * up
    coef_ref[5] = back * silu
    coef_ref[6] = silu * up


def add_kernel(mine_ref, recv_ref, out_ref, *tail_refs):
    total = mine_ref[...] + recv_ref[...]
    out_ref[...] = total
    for ref in tail_refs:
        ref[...] = total[total.shape[0] - ref.shape[0] :]


def carry_kernel(mine_ref, recv_ref, *refs):
    refs[-1][:2] = mine_ref[...] + recv_ref[...]
    if len(refs) == 2:
        refs[1][2:] = refs[0][...]


def key_kernel(scale, share, order, *refs):
    total_ref, sums_ref, sib_ref, tok_ref, new_ref, old_ref, vec_ref, grad_ref, coef_ref = refs[:9]
    *outs, up_ref, mid_ref = refs[9:]
    dim = tok_ref.shape[-1]
    half = dim // 2
    down_sums = sums_ref[...] + sib_ref[...]
    pieces = ((0, dim, 0), (dim, dim, 1), (2 * dim, half, 2), (2 * dim + half, half, 3))
    upper, carried = [], []
    for row, rows, slot in pieces:
        adj = total_ref[row : row + rows, :]
        new = new_ref[row : row + rows, :]
        if slot < 2:
            sums = jnp.sum(new * adj, axis=0, keepdims=True)
        else:
            sums = down_sums[slot - 2 : slot - 1]
        ratio = vec_ref[slot : slot + 1, :]
        cross = vec_ref[4 + slot : 5 + slot, :]
        inverse = vec_ref[8 + slot : 9 + slot, :]
        up_adj = adj * ratio - new * (sums * cross)
        direct = old_ref[row : row + rows, :] * (sums * inverse)
        upper.append(up_adj * scale)
        carried.append((up_adj + direct) * share + grad_ref[row : row + rows, :])
        up_ref[row : row + rows, :] = upper[-1]
    key, value = tok_ref[0], tok_ref[1]
    raw = exact_left(key, split(jnp.concatenate(upper[:2], axis=1)), NN)
    back = exact_left(value, split(jnp.concatenate(upper[2:], axis=1)), NT)
    gate, up = raw[:, :half], raw[:, half:]
    hidden = coef_ref[0] * gate + coef_ref[1] * up
    d_gate = coef_ref[2] * gate + coef_ref[3] * up + coef_ref[0] * back
    d_up = coef_ref[3] * gate + coef_ref[1] * back
    d_gate_up = exact_left(key, split(jnp.concatenate([d_gate, d_up], axis=1)), TN)
    d_down = exact_right(split(hidden), value, TN)
    mid_ref[0] = d_gate
    mid_ref[1] = d_up
    mid_ref[2] = hidden
    results = [
        d_gate_up[:, :half] + carried[0],
        d_gate_up[:, half:] + carried[1],
        d_down[:, :half] + carried[2],
        d_down[:, half:] + carried[3],
    ]
    if order is None:
        (out_ref,) = outs
        out_ref[3 * dim :, :] = jnp.zeros((PAD, half), F32)
        for (row, rows, slot), value in zip(pieces, results):
            out_ref[row : row + rows, :] = value
            if slot >= 2:
                out_ref[3 * dim + slot - 2 : 3 * dim + slot - 1, :] = jnp.sum(
                    value * old_ref[row : row + rows, :], axis=0, keepdims=True
                )
    else:
        halves = [[results[0][:half], results[1][:half], results[2]]]
        halves.append([results[0][half:], results[1][half:], results[3]])
        store_halves(halves, order, *outs)


def store_halves(halves, order, keep_ref, send_ref):
    bit = bit_of(order)

    def put(kept, sent):
        for index in range(3):
            keep_ref[index] = kept[index]
            send_ref[index] = sent[index]

    pl.when(bit)(functools.partial(put, halves[1], halves[0]))
    pl.when(jnp.logical_not(bit))(functools.partial(put, halves[0], halves[1]))


def halve_kernel(order, mine_ref, recv_ref, *outs):
    total = mine_ref[...] + recv_ref[...]
    if order is None:
        outs[0][...] = total
        return
    size = total.shape[1] // 2
    halves = [[total[m, at * size : (at + 1) * size] for m in range(3)] for at in range(2)]
    store_halves(halves, order, *outs)


def pair_kernel(mine_ref, other_ref, out_ref):
    out_ref[0] = mine_ref[...]
    out_ref[1] = other_ref[...]


def choose_kernel(tok_count, own_ref, moved_ref, out_ref):
    stays = working(tok_count)

    def put(source):
        out_ref[...] = source[...]

    pl.when(stays)(functools.partial(put, own_ref))
    pl.when(jnp.logical_not(stays))(functools.partial(put, moved_ref))


def init_out_kernel(tok_count, rs_orders, ag_orders, mine_ref, recv_ref, out_ref):
    dim = out_ref.shape[-1]
    half = dim // 2
    blocks = mine_ref.shape[0]
    size = mine_ref.shape[3]
    steps = len(ag_orders[0])
    stays = working(tok_count)
    for core in range(2):

        @pl.when(lax.axis_index("head") % 2 == core)
        def _():
            for flipped in range(2 * blocks):
                source = mine_ref if flipped < blocks else recv_ref
                where = flipped % blocks
                for slot in range(2):
                    which = core if slot == 0 else 1 - core
                    offset, first = 0, None
                    for at, (axis, mask) in enumerate(rs_orders[which]):
                        bit = (lax.axis_index(axis) // mask) % 2
                        step = ag_orders[core].index((axis, mask))
                        if (flipped >> step) & 1:
                            bit = 1 - bit
                        if at == 0:
                            first = bit
                        else:
                            offset = offset + bit * (dim >> (at + 1))
                    offset = pl.multiple_of(offset, size)
                    low = first * half + offset
                    for index in range(2):
                        out_ref[index, pl.ds(pl.multiple_of(low, size), size), which * half : (which + 1) * half] = (
                            source[where, slot, index]
                        )
                    rows = pl.ds(pl.multiple_of(which * half + offset, size), size)
                    pl.when(first == 0)(functools.partial(put_block, out_ref, rows, slice(0, half), source, where, slot))
                    pl.when(first == 1)(functools.partial(put_block, out_ref, rows, slice(half, dim), source, where, slot))


def put_block(out_ref, rows, lanes, source, where, slot):
    out_ref[2, rows, lanes] = source[where, slot, 2]


def token_kernel(tok_count, mid_ref, coef_ref, w_ref, up_ref, keep_ref, give_ref):
    dim = keep_ref.shape[-1]
    count = keep_ref.shape[1]
    w_gate_up, w_down = load_half(w_ref[...], dim)
    u_gate_up, u_down = load_half(up_ref[...], dim)
    left = jnp.concatenate([mid_ref[0], mid_ref[1]], axis=1)
    d_key = both_split(split(left), split(w_gate_up), NT)
    left = jnp.concatenate([coef_ref[4], coef_ref[5]], axis=1)
    d_key = d_key + both_split(split(left), split(u_gate_up), NT)
    left = jnp.concatenate([mid_ref[2], coef_ref[6]], axis=1)
    right = jnp.concatenate([w_down, u_down], axis=0)
    d_value = both_split(split(left), split(right), NN)

    def put(first, second):
        for index, value in enumerate((d_key, d_value)):
            first[index] = value[:count]
            second[index] = value[count:]

    stays = working(tok_count)
    pl.when(stays)(functools.partial(put, keep_ref, give_ref))
    pl.when(jnp.logical_not(stays))(functools.partial(put, give_ref, keep_ref))


def tokens_out_kernel(tok_count, own_ref, moved_ref, key_ref, value_ref):
    stays = working(tok_count)
    groups = own_ref.shape[0] // 2

    def put(source):
        for index in range(groups):
            key_ref[index] = source[2 * index].astype(key_ref.dtype)
            value_ref[index] = source[2 * index + 1].astype(value_ref.dtype)

    pl.when(stays)(functools.partial(put, own_ref))
    pl.when(jnp.logical_not(stays))(functools.partial(put, moved_ref))
    key_ref[groups] = jnp.zeros_like(key_ref[groups])
    value_ref[groups] = jnp.zeros_like(value_ref[groups])


def call(kernel, outs, *args, scratch=(), limit=16, flops=1, **kwargs):
    return pl.pallas_call(
        kernel,
        out_shape=outs,
        **kwargs,
        scratch_shapes=scratch,
        cost_estimate=pl.CostEstimate(flops=flops, bytes_accessed=1, transcendentals=0),
        compiler_params=pltpu.CompilerParams(vmem_limit_bytes=limit * 1024 * 1024),
    )(*args)


def shape(*dims, dtype=F32):
    return jax.ShapeDtypeStruct(dims, dtype)


def tie(array, after):
    return lax.optimization_barrier((array, after))[0]


def working(tok_count):
    return lax.axis_index("tok") // (tok_count // 2) == lax.axis_index("head") % 2


def bit_of(order):
    bits = [(lax.axis_index(axis) // mask) % 2 for axis, mask in order]
    return jnp.where(lax.axis_index("head") % 2 == 0, bits[0], bits[1]) == 1


def on_device(queries, keys, values, out_grad, fast_init, updates):
    tok_count = lax.axis_size("tok")
    head_count = lax.axis_size("head")
    vid_count = lax.axis_size("vid")
    _, groups, count, _, dim = queries.shape
    half = dim // 2
    rows = 3 * dim
    scale = float(count * tok_count) ** (-0.5)
    share = 2.0 / tok_count
    tok_dims = [("tok", 1 << i) for i in range((tok_count // 2).bit_length() - 1)]
    vid_dims = [("vid", 1 << i) for i in range(vid_count.bit_length() - 1)]
    assert len(tok_dims) >= 1 and 2 << len(tok_dims) == tok_count
    assert 1 << len(vid_dims) == vid_count and head_count % 2 == 0
    assert queries.shape[0] == 1 and queries.shape[3] == 1

    def stays_at(tok, head):
        return tok // (tok_count // 2) == head % 2

    def permute(array, goes):
        pairs = []
        for tok in range(tok_count):
            for head in range(head_count):
                for vid in range(vid_count):
                    there = goes(tok, head, vid)
                    if there is not None:
                        number = lambda t, h, v: (t * head_count + h) * vid_count + v
                        pairs.append((number(tok, head, vid), number(*there)))
        return lax.ppermute(array, ("tok", "head", "vid"), pairs)

    def meet(array, order):
        def goes(tok, head, vid):
            axis, mask = order[head % 2]
            return (tok ^ mask, head, vid) if axis == "tok" else (tok, head, vid ^ mask)

        return permute(array, goes)

    def sibling(array, from_staying=None):
        def goes(tok, head, vid):
            if from_staying is None or stays_at(tok, head) == from_staying:
                return (tok, head ^ 1, vid)

        return permute(array, goes)

    def spread(array):
        def goes(tok, head, vid):
            if stays_at(tok, head):
                return (tok, head ^ 1, vid)
            return (tok ^ (tok_count // 2), head, vid)

        return permute(array, goes)

    def swap(array):
        def goes(tok, head, vid):
            if not stays_at(tok, head):
                return (tok ^ (tok_count // 2), head ^ 1, vid)

        return permute(array, goes)

    def lend(array):
        def goes(tok, head, vid):
            if stays_at(tok, head):
                return (tok ^ (tok_count // 2), head, vid)
            return (tok, head ^ 1, vid)

        return permute(array, goes)

    flat = lambda array: array.reshape(groups, count, dim)
    q_all, k_all, v_all, c_all = (flat(a) for a in (queries, keys, values, out_grad))
    top = groups - 1
    init = fast_init.reshape(3, dim, dim)
    steps = updates.reshape(groups - 1, 3, dim, dim)

    def send(arrays, index, limit=16, whole=False):
        outs = [shape(2, count, dim)] * (len(arrays) // 2)
        return call(
            functools.partial(send_kernel, index, len(arrays)),
            outs + [shape(len(arrays), count, dim)] * whole,
            *arrays,
            limit=limit,
            in_specs=[pl.BlockSpec(memory_space=pltpu.HBM)] * len(arrays),
            scratch=[
                pltpu.VMEM((len(arrays), count, dim), BF16),
                pltpu.SemaphoreType.DMA((len(arrays),)),
            ],
        )

    own = {top: send([q_all, c_all], top, 60)}
    first = {top: [spread(own[top][0])]}
    init = tie(init, own[top][0])

    low_rows = top * rows + top * VEC
    low_rows += -low_rows % 8
    full, *halves = call(
        prep_kernel,
        [shape(top, 3, dim, dim)] + [shape(rows, half), shape(low_rows, half)] * 2,
        init,
        steps,
        in_specs=[pl.BlockSpec(memory_space=pltpu.HBM)] * 2,
        scratch=[
            pltpu.VMEM(init.shape, BF16),
            pltpu.VMEM(steps.shape, BF16),
            pltpu.SemaphoreType.DMA((groups,)),
        ],
    )

    def chosen(outs, mine, sent):
        return call(functools.partial(weights_kernel, tok_count), outs, mine, sibling(sent))

    (top_weights,) = chosen([shape(rows, half)], halves[0], halves[2])
    (query_grad,) = call(query_kernel, [shape(groups, count, dim, dtype=BF16)], q_all, c_all, init, full)

    def tokens(index, after):
        arrays = []
        if not isinstance(first[index], list):
            pairs = [shape(2, count, dim)] * len(own[index])
            first[index] = call(part_kernel, pairs, first[index], flops=4000000000)
        for mine, arrived in zip(own[index], first[index]):
            arrays += [mine, arrived, sibling(tie(arrived, after), True)]
        return arrays

    def scratch(index):
        return [pltpu.VMEM((2 * len(own[index]), 2 * count, dim), BF16)]

    both = 2 * count
    (payload,) = call(
        functools.partial(last_kernel, tok_count),
        [shape(rows + PAD, half)],
        *tokens(top, query_grad),
        top_weights,
        scratch=scratch(top),
    )
    weights = chosen(
        [shape(rows, half)] * top + [shape(VEC, half)] * top, halves[1], tie(halves[3], first[top][0])
    )
    factors = list(weights[top:])
    weights = [*weights[:top], top_weights]
    token_grads = []
    for index in reversed(range(top)):
        one = True
        own[index] = send([q_all, c_all, k_all, v_all], index, whole=one)
        if one:
            *own[index], whole = own[index]
            first[index] = spread(tie(whole, first[index + 1]))
        else:
            first[index] = [spread(tie(array, first[index + 1])) for array in own[index]]
        for at in range(len(tok_dims)):
            arrived = meet(payload, (tok_dims[at], tok_dims[at - 1]))
            if at + 1 < len(tok_dims):
                if at == 0 and token_grads:
                    arrived = tie(arrived, token_grads[-1])
                (payload,) = call(add_kernel, [shape(rows + PAD, half)], payload, arrived)
        grad, coef, keyed = call(
            functools.partial(pre_kernel, tok_count),
            [shape(rows, half), shape(7, both, half), shape(2, both, dim, dtype=BF16)],
            *tokens(index, payload),
            weights[index],
            scratch=scratch(index),
        )
        total, sums = call(add_kernel, [shape(rows + PAD, half), shape(PAD, half)], payload, arrived)
        if index > 0:
            out_shapes, order = [shape(rows + PAD, half)], None
        else:
            dims = tok_dims + vid_dims
            rs_orders = [dims, dims[-1:] + dims[:-1]]
            order = [rs_orders[0][0], rs_orders[1][0]]
            out_shapes = [shape(3, half, half)] * 2
        *outs, upper, mid = call(
            functools.partial(key_kernel, scale, share, order),
            out_shapes + [shape(rows, half), shape(3, both, half)],
            total,
            sums,
            sibling(sums),
            keyed,
            weights[index + 1],
            weights[index],
            factors[index],
            grad,
            coef,
        )
        payload = outs[0]
        keep, give = call(
            functools.partial(token_kernel, tok_count),
            [shape(2, count, dim)] * 2,
            mid,
            coef,
            weights[index],
            upper,
        )
        done = 2 * (top - index)
        (d_tokens,) = call(
            carry_kernel, [shape(done, count, dim)], keep, sibling(give), *token_grads[-1:]
        )
        token_grads.append(d_tokens)

    kept, sends = outs
    returned = swap(token_grads[-1])

    def wait(array, point):
        return tie(array, returned) if point == 5 else array

    for at in range(len(dims)):
        arrived = meet(sends, [order[at] for order in rs_orders])
        arrived = wait(arrived, at)
        if at + 1 < len(dims):
            out_shapes = [shape(3, kept.shape[1] // 2, half)] * 2
            order = [order[at + 1] for order in rs_orders]
            kept, sends = call(functools.partial(halve_kernel, order), out_shapes, kept, arrived)
        else:
            (kept,) = call(functools.partial(halve_kernel, None), [shape(*kept.shape)], kept, arrived)
    (pair,) = call(pair_kernel, [shape(2, *kept.shape)], kept, sibling(wait(kept, 2)))
    (block,) = call(
        functools.partial(choose_kernel, tok_count), [shape(*pair.shape)], pair, lend(pair)
    )
    block = wait(block[None], 3)
    ag_orders = [vid_dims + tok_dims, tok_dims + vid_dims]
    for at in range(len(dims)):
        arrived = wait(meet(block, [order[at] for order in ag_orders]), 4 + at)
        if at + 1 < len(dims):
            (pair,) = call(pair_kernel, [shape(2, *block.shape)], block, arrived)
            block = pair.reshape(2 * block.shape[0], *block.shape[1:])
    (init_grad,) = call(
        functools.partial(init_out_kernel, tok_count, rs_orders, ag_orders),
        [shape(3, dim, dim)],
        block,
        arrived,
    )
    key_grad, value_grad = call(
        functools.partial(tokens_out_kernel, tok_count),
        [shape(groups, count, dim, dtype=BF16)] * 2,
        token_grads[-1],
        returned,
    )
    back = lambda array: array.reshape(queries.shape)
    return back(query_grad), back(key_grad), back(value_grad), init_grad.reshape(fast_init.shape)


def solution(mesh):
    tokens = P("vid", None, "tok", "head", None)
    return jax.shard_map(
        on_device,
        mesh=mesh,
        in_specs=(
            tokens,
            tokens,
            tokens,
            tokens,
            P("head", None, None, None),
            P("vid", None, "head", None, None, None),
        ),
        out_specs=(tokens, tokens, tokens, P("head", None, None, None)),
        check_vma=False,
    )
```
